128 devices in a mesh: chan: 32 (over x, z_lo, y), sub: 4 (over z_hi, core).
Axes of the slice: x: 4, y: 4, z: 4 (z_hi: 2, z_lo: 2; z = z_hi * 2 + z_lo), core: 2. Of those that a mesh axis runs over, the one named last changes fastest.
Arguments:
- traces: bfloat16 [16384, 16384], P(('chan', 'sub')), may hold values from -6 to 6
- fan_mask: int32 [512, 16384], P('chan'), may hold values from 0 to 1, as said below
- band_edges: int32 [66], replicated, may hold values from 0 to 511, as said below
Outputs:
- cepstra: float32 [16, 64, 16384], P(None, None, ('chan', 'sub'))
The draws below stay inside these ranges and needn't reach their ends.
Inputs may be any that keep to these rules, and one draw needn't show every extreme that they name: `fan_mask`: 0 or 1 for each frequency bin and wavenumber index. `band_edges`: strictly increasing; the first is 0 and the last is 511.
All inputs are finite; a program needn't handle non-finite values.
Results may differ from the reference program's by a relative error of at most 0.006.
Values may be sent and summed in bfloat16 or wider, within the bound.
No kernel may reach another device: no remote copies, remote signals or barrier semaphores. Data moves between devices by JAX's collectives and lax.ppermute only.
A program may use at most 128 MiB of HBM per device.

```python
import math
import jax
import jax.numpy as jnp
from jax import lax

NCH = 16384
N1 = 128
N2 = 128
FLEN = 1024
NF = 512
NB = 64
FRAMES = 16
SAMPLES = 16384


def draw_fan_mask(key, part):
    key = jax.random.fold_in(key, 11)
    freq_index = jnp.arange(NF, dtype=jnp.int32)[:, None]
    wave_index = jnp.arange(NCH, dtype=jnp.int32)[None, :]
    folded = jnp.minimum(wave_index, NCH - wave_index)
    inside = folded * NF <= freq_index * (NCH // 2)
    rolled = jax.random.randint(key, (NF, NCH), 0, 8)
    return jnp.where(inside, rolled != 0, rolled == 0).astype(jnp.int32)


def draw_band_edges(key, part):
    key = jax.random.fold_in(key, 23)
    widest = (NF - 1) // (NB + 1)
    spacing = jax.random.randint(key, (NB + 1,), 1, widest + 1)
    running = jnp.concatenate([jnp.zeros((1,), jnp.int32), jnp.cumsum(spacing).astype(jnp.int32)])
    return (running * (NF - 1) // running[-1]).astype(jnp.int32)


def steps_of(own_key, extent, pieces, low, top_value):
    def one(position, parts):
        draws = jax.random.uniform(jax.random.fold_in(jax.random.fold_in(own_key, 6), position), (parts,), jnp.float32, low / len(pieces), top_value / len(pieces))
        return jnp.repeat(jnp.exp(draws), extent[position] // parts).reshape((-1,) + (1,) * (len(extent) - position - 1))

    gain = one(*pieces[0])
    for cut in pieces[1:]:
        gain = gain * one(*cut)
    return gain


def centred(rng, dims, spread, bound, shards=(), kind=jnp.bfloat16):
    loudness = steps_of(rng, dims, shards, -0.22, 0.18) if shards else 1.0
    values = jax.random.normal(rng, dims, jnp.float32) * spread * loudness
    return jnp.minimum(jnp.maximum(values, -bound), bound).astype(kind)


def setup_inputs(seed: int = 0) -> dict:
    streams_of = jax.random.split(jax.random.key(seed), 4)
    traces = centred(streams_of[0], (NCH, SAMPLES), 1.0, 6.0, ((0, 128),))
    fan_mask = draw_fan_mask(jax.random.fold_in(streams_of[3], 71), 0)
    band_edges = draw_band_edges(jax.random.fold_in(streams_of[3], 71), 0)
    return {"traces": traces, "fan_mask": fan_mask, "band_edges": band_edges}


energy_floor = 0.05


def time_table(frame_len, bin_count):
    sample_index = jnp.arange(frame_len, dtype=jnp.int32)
    freq_index = jnp.arange(bin_count, dtype=jnp.int32)
    hann_window = 0.5 - 0.5 * jnp.cos((2.0 * math.pi / frame_len) * sample_index.astype(jnp.float32))
    phases = (2.0 * math.pi / frame_len) * ((freq_index[:, None] * sample_index[None, :]) % frame_len).astype(jnp.float32)
    factor = (0.375 * frame_len) ** -0.5
    real_part = jnp.cos(phases) * hann_window[None, :] * factor
    imag_part = -jnp.sin(phases) * hann_window[None, :] * factor
    return jnp.stack([real_part, imag_part], axis=0).astype(jnp.bfloat16)


def dft_block(out_index, in_index, length, sign_value):
    phases = (2.0 * math.pi / length) * ((out_index[:, None] * in_index[None, :]) % length).astype(jnp.float32)
    factor = length ** -0.5
    real_part = jnp.cos(phases) * factor
    imag_part = sign_value * jnp.sin(phases) * factor
    top_half = jnp.stack([real_part, -imag_part], axis=1)
    bottom = jnp.stack([imag_part, real_part], axis=1)
    return jnp.stack([top_half, bottom], axis=0).astype(jnp.bfloat16)


def twiddle(out_index, in_index, total_len, sign_value):
    phases = (2.0 * math.pi / total_len) * ((out_index[:, None] * in_index[None, :]) % total_len).astype(jnp.float32)
    return jnp.cos(phases), sign_value * jnp.sin(phases)


def rotate(values, cos_part, sin_part):
    real_part = values[0] * cos_part - values[1] * sin_part
    imag_part = values[0] * sin_part + values[1] * cos_part
    return jnp.stack([real_part, imag_part], axis=0)


def band_weights(band_edges, bin_count):
    bounds = band_edges.astype(jnp.float32)
    freq_value = jnp.arange(bin_count, dtype=jnp.int32).astype(jnp.float32)[None, :]
    lower_edge = bounds[:-2, None]
    middle = bounds[1:-1, None]
    upper_edge = bounds[2:, None]
    rising = (freq_value - lower_edge) / (middle - lower_edge)
    falling = (upper_edge - freq_value) / (upper_edge - middle)
    return jnp.maximum(jnp.minimum(rising, falling), 0.0).astype(jnp.bfloat16)


def cosine_table(band_count):
    ordering = jnp.arange(band_count, dtype=jnp.int32)
    phases = (math.pi / (2 * band_count)) * ((ordering[:, None] * (2 * ordering[None, :] + 1)) % (4 * band_count)).astype(jnp.float32)
    weight = jnp.where(ordering == 0, (1.0 / band_count) ** 0.5, (2.0 / band_count) ** 0.5)
    return jnp.cos(phases) * weight[:, None]


def reference(traces, fan_mask, band_edges):
    f32 = jnp.float32
    table_time = time_table(FLEN, NF).astype(f32)
    first_index = jnp.arange(N1, dtype=jnp.int32)
    second_index = jnp.arange(N2, dtype=jnp.int32)
    first_table = dft_block(second_index, second_index, N2, -1.0).astype(f32)
    second_table = dft_block(first_index, first_index, N1, -1.0).astype(f32)
    third_table = dft_block(first_index, first_index, N1, 1.0).astype(f32)
    fourth_table = dft_block(second_index, second_index, N2, 1.0).astype(f32)
    fwd_cos, fwd_sin = twiddle(second_index, first_index, NCH, -1.0)
    inv_cos, inv_sin = twiddle(second_index, first_index, NCH, 1.0)
    mask_cells = jnp.transpose(fan_mask.reshape(NF, N1, N2), (1, 2, 0))
    weights = band_weights(band_edges, NF).astype(f32)
    cosine = cosine_table(NB)
    frame_rows = traces.reshape(NCH, FRAMES, FLEN)

    def one_frame(frame_index):
        samples = lax.dynamic_index_in_dim(frame_rows, frame_index, 1, keepdims=False).astype(f32)
        spectrum = jnp.einsum("xft,ct->xcf", table_time, samples).astype(jnp.bfloat16)
        cells = spectrum.reshape(2, N2, N1, NF).astype(f32)
        first_sum = jnp.einsum("ykxc,xcaf->ykaf", first_table, cells)
        section_one = rotate(first_sum, fwd_cos[:, :, None], fwd_sin[:, :, None]).astype(jnp.bfloat16)
        section_two = jnp.einsum("ykxa,xuaf->ykuf", second_table, section_one.astype(f32)).astype(jnp.bfloat16)
        kept_cells = jnp.where(mask_cells[None] > 0, section_two, jnp.zeros_like(section_two))
        inverse_sum = jnp.einsum("ycxk,xkuf->yucf", third_table, kept_cells.astype(f32))
        section_three = rotate(inverse_sum, inv_cos[:, :, None], inv_sin[:, :, None]).astype(jnp.bfloat16)
        filtered = jnp.einsum("ydxu,xucf->ydcf", fourth_table, section_three.astype(f32)).astype(jnp.bfloat16)
        values = filtered.reshape(2, NCH, NF).astype(f32)
        power = (values[0] * values[0] + values[1] * values[1]).astype(jnp.bfloat16)
        energy = jnp.einsum("bf,cf->bc", weights, power.astype(f32))
        logs = jnp.log(jnp.maximum(energy, energy_floor))
        return jnp.dot(cosine, logs, precision=lax.Precision.HIGHEST)

    return lax.map(one_frame, jnp.arange(FRAMES, dtype=jnp.int32))
```

```python
import functools
import math

import jax
import jax.numpy as jnp
import ml_dtypes
import numpy as np
from jax import lax
from jax.experimental import pallas as pl
from jax.experimental.pallas import tpu as pltpu
from jax.sharding import PartitionSpec as P

NCH = 16384
N1 = 128
N2 = 128
FLEN = 1024
NF = 512
NB = 64
FRAMES = 16
HALF = FRAMES // 2

energy_floor = 0.05


def time_table(devices):
    bins = NF // devices
    t = np.arange(FLEN)
    f = np.arange(NF)
    hann = 0.5 - 0.5 * np.cos(2.0 * math.pi * t / FLEN)
    phases = 2.0 * math.pi / FLEN * ((f[:, None] * t[None, :]) % FLEN)
    factor = (0.375 * FLEN) ** -0.5
    table = np.stack([np.cos(phases), -np.sin(phases)], axis=0) * (hann * factor)
    table = table.reshape(2, devices, bins, FLEN).transpose(1, 0, 2, 3)
    return table.reshape(2 * NF, FLEN).astype(ml_dtypes.bfloat16)


def dft_parts(length, sign):
    n = np.arange(length)
    phases = 2.0 * math.pi / length * ((n[:, None] * n[None, :]) % length)
    factor = length**-0.5
    return np.cos(phases) * factor, sign * np.sin(phases) * factor


def left_table(length, sign):
    re, im = dft_parts(length, sign)
    return np.block([[re, -im], [im, re]]).astype(ml_dtypes.bfloat16)


def right_table(length, sign):
    re, im = dft_parts(length, sign)
    return np.block([[re, im], [-im, re]]).astype(ml_dtypes.bfloat16)


def twiddle(sign):
    q = np.arange(N2)
    a = np.arange(N1)
    phases = 2.0 * math.pi / NCH * ((q[:, None] * a[None, :]) % NCH)
    return np.stack([np.cos(phases), sign * np.sin(phases)]).astype(np.float32)


def cosine_table():
    j = np.arange(NB)
    phases = math.pi / (2 * NB) * ((j[:, None] * (2 * j[None, :] + 1)) % (4 * NB))
    weight = np.where(j == 0, (1.0 / NB) ** 0.5, (2.0 / NB) ** 0.5)
    return (np.cos(phases) * weight[:, None]).astype(np.float32)


def band_weights(band_edges):
    bounds = band_edges.astype(jnp.float32)
    freq = jnp.arange(NF, dtype=jnp.int32).astype(jnp.float32)[None, :]
    low, middle, high = bounds[:-2, None], bounds[1:-1, None], bounds[2:, None]
    rising = (freq - low) / (middle - low)
    falling = (high - freq) / (high - middle)
    return jnp.maximum(jnp.minimum(rising, falling), 0.0).astype(jnp.bfloat16)


def spectrum_kernel(devices, table_ref, low_ref, high_ref, out_ref):
    rows = 2 * NF // devices
    low, high = low_ref[...], high_ref[...]
    samples = jnp.concatenate(
        [low[:, :FLEN], low[:, FLEN:], high[:, :FLEN], high[:, FLEN:]], axis=0
    )
    step = 256
    for start in range(0, 2 * NF, step):
        part = lax.dot_general(
            table_ref[start : start + step, :],
            samples,
            (((1,), (1,)), ((), ())),
            preferred_element_type=jnp.float32,
        )
        part = part.reshape(step // rows, rows, 4 * N1)
        both = jnp.concatenate([part[:, :, : 2 * N1], part[:, :, 2 * N1 :]], axis=1)
        out_ref[start // rows : (start + step) // rows] = both.astype(jnp.bfloat16)


def sections_kernel(
    bins,
    cells_ref,
    first_ref,
    second_ref,
    third_ref,
    fourth_ref,
    forward_ref,
    inverse_ref,
    mask_ref,
    power_ref,
    cells_f32,
    power_f32,
):
    rows = 4 * bins
    dot = functools.partial(jnp.dot, preferred_element_type=jnp.float32)
    bf16 = jnp.bfloat16
    for m in range(2):
        part = cells_ref[:, :, m * N1 : (m + 1) * N1].astype(jnp.float32)
        cells_f32[m] = part.reshape(N2 * rows, N1)
    fwd_cos, fwd_sin = forward_ref[0], forward_ref[1]
    inv_cos, inv_sin = inverse_ref[0], inverse_ref[1]
    for m in range(2):
        for half in range(2):
            for pair in range(bins // 2):
                bin_pair = (2 * pair, 2 * pair + 1)

                def cell(x, f):
                    at = half * 2 * bins + x * bins + f
                    return cells_f32[m, pl.ds(at, N2, stride=rows), :].astype(bf16)

                cells = jnp.concatenate(
                    [
                        jnp.concatenate([cell(x, f) for f in bin_pair], axis=1)
                        for x in range(2)
                    ],
                    axis=0,
                )
                summed = dot(first_ref[...], cells)
                rotated = []
                for i in range(2):
                    re = summed[:N2, i * N1 : (i + 1) * N1]
                    im = summed[N2:, i * N1 : (i + 1) * N1]
                    rotated.append(
                        jnp.concatenate(
                            [
                                (re * fwd_cos - im * fwd_sin).astype(bf16),
                                (re * fwd_sin + im * fwd_cos).astype(bf16),
                            ],
                            axis=1,
                        )
                    )
                section = dot(jnp.concatenate(rotated, axis=0), second_ref[...]).astype(bf16)
                masks = []
                for f in bin_pair:
                    mask = mask_ref[f]
                    masks.append(jnp.concatenate([mask, mask], axis=1))
                kept = section * jnp.concatenate(masks, axis=0)
                back = dot(kept, third_ref[...])
                re_parts, im_parts = [], []
                for i in range(2):
                    re = back[i * N2 : (i + 1) * N2, :N1]
                    im = back[i * N2 : (i + 1) * N2, N1:]
                    re_parts.append((re * inv_cos - im * inv_sin).astype(bf16))
                    im_parts.append((re * inv_sin + im * inv_cos).astype(bf16))
                turned = jnp.concatenate(
                    [
                        jnp.concatenate(re_parts, axis=1),
                        jnp.concatenate(im_parts, axis=1),
                    ],
                    axis=0,
                )
                filtered = dot(fourth_ref[...], turned).astype(bf16).astype(jnp.float32)
                re, im = filtered[:N2], filtered[N2:]
                power = re * re + im * im
                for i, f in enumerate(bin_pair):
                    at = m * 2 * bins + half * bins + f
                    power_f32[pl.ds(at, N2, stride=rows), :] = power[:, i * N1 : (i + 1) * N1]
    power_ref[...] = power_f32[...].reshape(N2, rows, N1).astype(bf16)


def cepstra_kernel(bins, power_ref, weights_ref, cosine_ref, out_ref, power_f32):
    rows = 4 * bins
    power_f32[...] = power_ref[...].astype(jnp.float32).reshape(N2 * rows, N1)
    columns = []
    for half in range(2):
        for m in range(2):
            at = m * 2 * bins + half * bins
            columns.append(
                jnp.concatenate(
                    [
                        power_f32[pl.ds(at + f, N2, stride=rows), :].astype(jnp.bfloat16)
                        for f in range(bins)
                    ],
                    axis=0,
                )
            )
    power = jnp.concatenate(columns, axis=1)
    energy = jnp.dot(weights_ref[...], power, preferred_element_type=jnp.float32)
    logs = jnp.log(jnp.maximum(energy, energy_floor))
    cepstra = jnp.dot(
        cosine_ref[...],
        logs,
        precision=lax.Precision.HIGHEST,
        preferred_element_type=jnp.float32,
    )
    for half in range(2):
        for m in range(2):
            at = (half * 2 + m) * N1
            out_ref[half, m] = cepstra[:, at : at + N1]


def whole(shape):
    return pl.BlockSpec(shape, lambda i: (0,) * len(shape))


VMEM_LIMIT = 48 * 1024 * 1024


def shards(traces, fan_mask, band_edges):
    axes = ("chan", "sub")
    devices = lax.axis_size("chan") * lax.axis_size("sub")
    sub_count = lax.axis_size("sub")
    bins = NF // devices
    rows = 4 * bins
    bf16 = jnp.bfloat16
    params = pltpu.CompilerParams(vmem_limit_bytes=VMEM_LIMIT)

    spectrum = pl.pallas_call(
        functools.partial(spectrum_kernel, devices),
        grid=(HALF // 2,),
        in_specs=[
            whole((2 * NF, FLEN)),
            pl.BlockSpec((N1, 2 * FLEN), lambda i: (0, i)),
            pl.BlockSpec((N1, 2 * FLEN), lambda i: (0, i + HALF // 2)),
        ],
        out_specs=pl.BlockSpec((devices, rows, 2 * N1), lambda i: (0, 0, i)),
        out_shape=jax.ShapeDtypeStruct((devices, rows, HALF * N1), bf16),
        compiler_params=params,
        name="spectrum",
    )(jnp.asarray(time_table(devices)), traces, traces)

    cells = lax.all_to_all(spectrum, axes, split_axis=0, concat_axis=0, tiled=True)

    mask = lax.dynamic_slice_in_dim(fan_mask, lax.axis_index("sub") * bins, bins, 0)
    mask = jnp.transpose(mask.reshape(bins, N1, N2), (0, 2, 1))
    mask = (mask > 0).astype(bf16)

    power = pl.pallas_call(
        functools.partial(sections_kernel, bins),
        grid=(HALF // 2,),
        in_specs=[
            pl.BlockSpec((N2, rows, 2 * N1), lambda i: (0, 0, i)),
            whole((2 * N2, 2 * N2)),
            whole((2 * N1, 2 * N1)),
            whole((2 * N1, 2 * N1)),
            whole((2 * N2, 2 * N2)),
            whole((2, N2, N1)),
            whole((2, N2, N1)),
            whole((bins, N2, N1)),
        ],
        out_specs=pl.BlockSpec((N2, rows, N1), lambda i: (0, 0, i)),
        out_shape=jax.ShapeDtypeStruct((N2, rows, HALF // 2 * N1), bf16),
        scratch_shapes=[
            pltpu.VMEM((2, N2 * rows, N1), jnp.float32),
            pltpu.VMEM((N2 * rows, N1), jnp.float32),
        ],
        compiler_params=params,
        name="sections",
    )(
        cells,
        jnp.asarray(left_table(N2, -1.0)),
        jnp.asarray(right_table(N1, -1.0)),
        jnp.asarray(right_table(N1, 1.0)),
        jnp.asarray(left_table(N2, 1.0)),
        jnp.asarray(twiddle(-1.0)),
        jnp.asarray(twiddle(1.0)),
        mask,
    )

    returned = lax.all_to_all(power, axes, split_axis=0, concat_axis=0, tiled=True)

    weights = band_weights(band_edges).reshape(NB, devices, bins)
    weights = jnp.transpose(weights, (0, 2, 1)).reshape(NB, NF)
    cepstra = pl.pallas_call(
        functools.partial(cepstra_kernel, bins),
        grid=(HALF // 2,),
        in_specs=[
            pl.BlockSpec((devices, rows, N1), lambda i: (0, 0, i)),
            whole((NB, NF)),
            whole((NB, NB)),
        ],
        out_specs=pl.BlockSpec((2, 2, NB, N1), lambda i: (0, i, 0, 0)),
        out_shape=jax.ShapeDtypeStruct((2, HALF, NB, N1), jnp.float32),
        scratch_shapes=[pltpu.VMEM((devices * rows, N1), jnp.float32)],
        compiler_params=params,
        name="cepstra",
    )(returned, weights, jnp.asarray(cosine_table()))
    return cepstra.reshape(FRAMES, NB, N1)


def solution(mesh):
    in_specs = (P(("chan", "sub"), None), P("chan", None), P())
    out_specs = P(None, None, ("chan", "sub"))
    return jax.shard_map(shards, mesh=mesh, in_specs=in_specs, out_specs=out_specs, check_vma=False)
```

```python
import functools
import math

import jax
import jax.numpy as jnp
import ml_dtypes
import numpy as np
from jax import lax
from jax.experimental import pallas as pl
from jax.experimental.pallas import tpu as pltpu
from jax.sharding import PartitionSpec as P

NCH = 16384
N1 = 128
N2 = 128
FLEN = 1024
NF = 512
NB = 64
FRAMES = 16
HALF = FRAMES // 2

energy_floor = 0.05


def time_table(devices):
    bins = NF // devices
    t = np.arange(FLEN)
    f = np.arange(NF)
    hann = 0.5 - 0.5 * np.cos(2.0 * math.pi * t / FLEN)
    phases = 2.0 * math.pi / FLEN * ((f[:, None] * t[None, :]) % FLEN)
    factor = (0.375 * FLEN) ** -0.5
    table = np.stack([np.cos(phases), -np.sin(phases)], axis=0) * (hann * factor)
    table = table.reshape(2, devices, bins, FLEN).transpose(1, 0, 2, 3)
    return table.reshape(2 * NF, FLEN).astype(ml_dtypes.bfloat16)


def dft_parts(length, sign):
    n = np.arange(length)
    phases = 2.0 * math.pi / length * ((n[:, None] * n[None, :]) % length)
    factor = length**-0.5
    return np.cos(phases) * factor, sign * np.sin(phases) * factor


def left_table(length, sign):
    re, im = dft_parts(length, sign)
    return np.block([[re, -im], [im, re]]).astype(ml_dtypes.bfloat16)


def right_table(length, sign):
    re, im = dft_parts(length, sign)
    return np.block([[re, im], [-im, re]]).astype(ml_dtypes.bfloat16)


def twiddle(sign):
    q = np.arange(N2)
    a = np.arange(N1)
    phases = 2.0 * math.pi / NCH * ((q[:, None] * a[None, :]) % NCH)
    return np.stack([np.cos(phases), sign * np.sin(phases)]).astype(np.float32)


def cosine_table():
    j = np.arange(NB)
    phases = math.pi / (2 * NB) * ((j[:, None] * (2 * j[None, :] + 1)) % (4 * NB))
    weight = np.where(j == 0, (1.0 / NB) ** 0.5, (2.0 / NB) ** 0.5)
    return (np.cos(phases) * weight[:, None]).astype(np.float32)


def band_weights(band_edges):
    bounds = band_edges.astype(jnp.float32)
    freq = jnp.arange(NF, dtype=jnp.int32).astype(jnp.float32)[None, :]
    low, middle, high = bounds[:-2, None], bounds[1:-1, None], bounds[2:, None]
    rising = (freq - low) / (middle - low)
    falling = (high - freq) / (high - middle)
    return jnp.maximum(jnp.minimum(rising, falling), 0.0).astype(jnp.bfloat16)


def row_order(bins):
    rows = 4 * bins
    group = 256 // rows
    order = np.zeros((256, 256))
    for r in range(rows):
        for b in range(group):
            order[r * group + b, b * rows + r] = 1.0
    return order.astype(ml_dtypes.bfloat16)


def spectrum_kernel(
    devices, chunks, parts, table_hbm, traces_hbm, out_hbm, table, traces, out, table_sem, traces_sem, out_sem
):
    rows = 2 * NF // devices
    height = 2 * NF // parts
    owners = devices // parts
    width = 2 * FLEN

    def table_copy(j):
        at = pl.ds(j * height, height)
        return pltpu.make_async_copy(table_hbm.at[at], table.at[at], table_sem.at[j])

    def traces_copy(i, half):
        at = pl.ds((half * chunks + i) * width, width)
        return pltpu.make_async_copy(
            traces_hbm.at[:, at], traces.at[i, half], traces_sem.at[i, half]
        )

    def out_copy(i, j):
        at = (pl.ds(j * owners, owners), slice(None), pl.ds(i * 2 * N1, 2 * N1))
        return pltpu.make_async_copy(out.at[at], out_hbm.at[at], out_sem.at[i, j])

    traces_copy(0, 0).start()
    table_copy(0).start()
    traces_copy(0, 1).start()
    for j in range(1, parts):
        table_copy(j).start()
    for i in range(1, chunks):
        for half in range(2):
            traces_copy(i, half).start()
    for i in range(chunks):
        for half in range(2):
            traces_copy(i, half).wait()
        low, high = traces[i, 0], traces[i, 1]
        samples = jnp.concatenate(
            [low[:, :FLEN], low[:, FLEN:], high[:, :FLEN], high[:, FLEN:]], axis=0
        )
        for j in range(parts):
            if i == 0:
                table_copy(j).wait()
            part = lax.dot_general(
                table[j * height : (j + 1) * height, :],
                samples,
                (((1,), (1,)), ((), ())),
                preferred_element_type=jnp.float32,
            )
            part = part.reshape(owners, rows, 4 * N1)
            both = jnp.concatenate([part[:, :, : 2 * N1], part[:, :, 2 * N1 :]], axis=1)
            out[j * owners : (j + 1) * owners, :, i * 2 * N1 : (i + 1) * 2 * N1] = both.astype(
                jnp.bfloat16
            )
            out_copy(i, j).start()
    for i in range(chunks):
        for j in range(parts):
            out_copy(i, j).wait()


def sections_kernel(
    bins,
    cells_ref,
    order_ref,
    first_ref,
    second_ref,
    third_ref,
    fourth_ref,
    forward_ref,
    inverse_ref,
    mask_ref,
    power_ref,
    cells,
    turned,
    kept,
    back,
    power_f32,
):
    rows = 4 * bins
    group = 256 // rows
    count = 4 * bins
    step = 2
    bf16 = jnp.bfloat16
    dot = functools.partial(jnp.dot, preferred_element_type=jnp.float32)
    for g in range(N2 // group):
        ordered = cells_ref[g * group : (g + 1) * group].reshape(256, 2 * N1)
        ordered = dot(order_ref[...], ordered).astype(bf16)
        for r in range(rows):
            half, x, f = r // (2 * bins), r // bins % 2, r % bins
            for m in range(2):
                n = (m * 2 + half) * bins + f
                cells[
                    x * N2 + g * group : x * N2 + (g + 1) * group, n * N1 : (n + 1) * N1
                ] = ordered[r * group : (r + 1) * group, m * N1 : (m + 1) * N1]
    fwd_cos, fwd_sin = forward_ref[0], forward_ref[1]
    for n0 in range(0, count, step):
        summed = dot(first_ref[...], cells[:, n0 * N1 : (n0 + step) * N1])
        for i in range(step):
            n = n0 + i
            re = summed[:N2, i * N1 : (i + 1) * N1]
            im = summed[N2:, i * N1 : (i + 1) * N1]
            turned[n * N2 : (n + 1) * N2, :N1] = (re * fwd_cos - im * fwd_sin).astype(bf16)
            turned[n * N2 : (n + 1) * N2, N1:] = (re * fwd_sin + im * fwd_cos).astype(bf16)
    for n0 in range(0, count, step):
        section = dot(turned[n0 * N2 : (n0 + step) * N2, :], second_ref[...]).astype(bf16)
        for i in range(step):
            n = n0 + i
            mask = mask_ref[n % bins]
            for x in range(2):
                kept[n * N2 : (n + 1) * N2, x * N1 : (x + 1) * N1] = (
                    section[i * N2 : (i + 1) * N2, x * N1 : (x + 1) * N1] * mask
                )
    inv_cos, inv_sin = inverse_ref[0], inverse_ref[1]
    for n0 in range(0, count, step):
        summed = dot(kept[n0 * N2 : (n0 + step) * N2, :], third_ref[...])
        for i in range(step):
            n = n0 + i
            re = summed[i * N2 : (i + 1) * N2, :N1]
            im = summed[i * N2 : (i + 1) * N2, N1:]
            back[:N2, n * N1 : (n + 1) * N1] = (re * inv_cos - im * inv_sin).astype(bf16)
            back[N2:, n * N1 : (n + 1) * N1] = (re * inv_sin + im * inv_cos).astype(bf16)
    for n0 in range(0, count, step):
        filtered = dot(fourth_ref[...], back[:, n0 * N1 : (n0 + step) * N1])
        filtered = filtered.astype(bf16).astype(jnp.float32)
        power = filtered[:N2] * filtered[:N2] + filtered[N2:] * filtered[N2:]
        for i in range(step):
            power_f32[pl.ds(n0 + i, N2, stride=rows), :] = power[:, i * N1 : (i + 1) * N1]
    power_ref[...] = power_f32[...].reshape(N2, rows, N1).astype(bf16)


def cepstra_kernel(power_ref, weights_ref, cosine_ref, out_ref):
    sources, rows, lanes = power_ref.shape
    power = power_ref[...].reshape(sources * rows, lanes)
    energy = jnp.dot(weights_ref[...], power, preferred_element_type=jnp.float32)
    logs = jnp.log(jnp.maximum(energy, energy_floor))
    for k in range(4):
        cepstra = jnp.dot(
            cosine_ref[...],
            logs[k * NB : (k + 1) * NB],
            precision=lax.Precision.HIGHEST,
            preferred_element_type=jnp.float32,
        )
        m, half = k // 2, k % 2
        for i in range(lanes // N1):
            out_ref[half, 2 * i + m] = cepstra[:, i * N1 : (i + 1) * N1]


def whole(shape):
    return pl.BlockSpec(shape, lambda i: (0,) * len(shape))


VMEM_LIMIT = 48 * 1024 * 1024


def shards(traces, fan_mask, band_edges):
    axes = ("chan", "sub")
    devices = lax.axis_size("chan") * lax.axis_size("sub")
    sub_count = lax.axis_size("sub")
    bins = NF // devices
    rows = 4 * bins
    bf16 = jnp.bfloat16
    params = pltpu.CompilerParams(vmem_limit_bytes=VMEM_LIMIT)

    chunks, parts = HALF // 2, 4
    spectrum = pl.pallas_call(
        functools.partial(spectrum_kernel, devices, chunks, parts),
        in_specs=[pl.BlockSpec(memory_space=pl.ANY)] * 2,
        out_specs=pl.BlockSpec(memory_space=pl.ANY),
        out_shape=jax.ShapeDtypeStruct((devices, rows, HALF * N1), bf16),
        scratch_shapes=[
            pltpu.VMEM((2 * NF, FLEN), bf16),
            pltpu.VMEM((chunks, 2, N1, 2 * FLEN), bf16),
            pltpu.VMEM((devices, rows, HALF * N1), bf16),
            pltpu.SemaphoreType.DMA((parts,)),
            pltpu.SemaphoreType.DMA((chunks, 2)),
            pltpu.SemaphoreType.DMA((chunks, parts)),
        ],
        compiler_params=params,
        name="spectrum",
    )(jnp.asarray(time_table(devices)), traces)

    cells = lax.all_to_all(spectrum, axes, split_axis=0, concat_axis=0, tiled=True)

    mask = lax.dynamic_slice_in_dim(fan_mask, lax.axis_index("sub") * bins, bins, 0)
    mask = jnp.transpose(mask.reshape(bins, N1, N2), (0, 2, 1))
    mask = (mask > 0).astype(bf16)

    power = pl.pallas_call(
        functools.partial(sections_kernel, bins),
        grid=(HALF // 2,),
        in_specs=[
            pl.BlockSpec((N2, rows, 2 * N1), lambda i: (0, 0, i)),
            whole((256, 256)),
            whole((2 * N2, 2 * N2)),
            whole((2 * N1, 2 * N1)),
            whole((2 * N1, 2 * N1)),
            whole((2 * N2, 2 * N2)),
            whole((2, N2, N1)),
            whole((2, N2, N1)),
            whole((bins, N2, N1)),
        ],
        out_specs=pl.BlockSpec((N2, rows, N1), lambda i: (0, 0, i)),
        out_shape=jax.ShapeDtypeStruct((N2, rows, HALF // 2 * N1), bf16),
        scratch_shapes=[
            pltpu.VMEM((2 * N2, rows * N1), bf16),
            pltpu.VMEM((rows * N2, 2 * N1), bf16),
            pltpu.VMEM((rows * N2, 2 * N1), bf16),
            pltpu.VMEM((2 * N2, rows * N1), bf16),
            pltpu.VMEM((N2 * rows, N1), jnp.float32),
        ],
        compiler_params=params,
        name="sections",
    )(
        cells,
        jnp.asarray(row_order(bins)),
        jnp.asarray(left_table(N2, -1.0)),
        jnp.asarray(right_table(N1, -1.0)),
        jnp.asarray(right_table(N1, 1.0)),
        jnp.asarray(left_table(N2, 1.0)),
        jnp.asarray(twiddle(-1.0)),
        jnp.asarray(twiddle(1.0)),
        mask,
    )

    returned = lax.all_to_all(power, axes, split_axis=0, concat_axis=0, tiled=True)

    weights = band_weights(band_edges).reshape(1, NB, devices, 1, bins)
    same = jnp.eye(4, dtype=bool)[:, None, None, :, None]
    weights = jnp.where(same, weights, jnp.zeros((), bf16)).reshape(4 * NB, devices * rows)
    cepstra = pl.pallas_call(
        cepstra_kernel,
        in_specs=[pl.BlockSpec(memory_space=pltpu.VMEM)] * 3,
        out_specs=pl.BlockSpec(memory_space=pltpu.VMEM),
        out_shape=jax.ShapeDtypeStruct((2, HALF, NB, N1), jnp.float32),
        compiler_params=params,
        name="cepstra",
    )(returned, weights, jnp.asarray(cosine_table()))
    return cepstra.reshape(FRAMES, NB, N1)


def solution(mesh):
    in_specs = (P(("chan", "sub"), None), P("chan", None), P())
    out_specs = P(None, None, ("chan", "sub"))
    return jax.shard_map(shards, mesh=mesh, in_specs=in_specs, out_specs=out_specs, check_vma=False)
```

```python
import functools
import math

import jax
import jax.numpy as jnp
import ml_dtypes
import numpy as np
from jax import lax
from jax.experimental import pallas as pl
from jax.experimental.pallas import tpu as pltpu
from jax.sharding import PartitionSpec as P

NCH = 16384
N1 = 128
N2 = 128
FLEN = 1024
NF = 512
NB = 64
FRAMES = 16
HALF = FRAMES // 2

energy_floor = 0.05


def time_table(devices):
    bins = NF // devices
    t = np.arange(FLEN)
    f = np.arange(NF)
    hann = 0.5 - 0.5 * np.cos(2.0 * math.pi * t / FLEN)
    phases = 2.0 * math.pi / FLEN * ((f[:, None] * t[None, :]) % FLEN)
    factor = (0.375 * FLEN) ** -0.5
    table = np.stack([np.cos(phases), -np.sin(phases)], axis=0) * (hann * factor)
    table = table.reshape(2, devices, bins, FLEN).transpose(1, 0, 2, 3)
    return table.reshape(2 * NF, FLEN).astype(ml_dtypes.bfloat16)


def dft_parts(length, sign):
    n = np.arange(length)
    phases = 2.0 * math.pi / length * ((n[:, None] * n[None, :]) % length)
    factor = length**-0.5
    return np.cos(phases) * factor, sign * np.sin(phases) * factor


def left_table(length, sign):
    re, im = dft_parts(length, sign)
    return np.block([[re, -im], [im, re]]).astype(ml_dtypes.bfloat16)


def right_table(length, sign):
    re, im = dft_parts(length, sign)
    return np.block([[re, im], [-im, re]]).astype(ml_dtypes.bfloat16)


def twiddle(sign):
    q = np.arange(N2)
    a = np.arange(N1)
    phases = 2.0 * math.pi / NCH * ((q[:, None] * a[None, :]) % NCH)
    return np.stack([np.cos(phases), sign * np.sin(phases)]).astype(np.float32)


def cosine_table():
    j = np.arange(NB)
    phases = math.pi / (2 * NB) * ((j[:, None] * (2 * j[None, :] + 1)) % (4 * NB))
    weight = np.where(j == 0, (1.0 / NB) ** 0.5, (2.0 / NB) ** 0.5)
    return (np.cos(phases) * weight[:, None]).astype(np.float32)


def band_weights(band_edges):
    bounds = band_edges.astype(jnp.float32)
    freq = jnp.arange(NF, dtype=jnp.int32).astype(jnp.float32)[None, :]
    low, middle, high = bounds[:-2, None], bounds[1:-1, None], bounds[2:, None]
    rising = (freq - low) / (middle - low)
    falling = (high - freq) / (high - middle)
    return jnp.maximum(jnp.minimum(rising, falling), 0.0).astype(jnp.bfloat16)


def spectrum_kernel(
    devices,
    chunks,
    parts,
    table_hbm,
    traces_hbm,
    out_hbm,
    table,
    traces,
    out,
    table_sem,
    traces_sem,
    out_sem,
):
    rows = 2 * NF // devices
    height = 2 * NF // parts
    owners = devices // parts
    frames = HALF // chunks
    width = frames * FLEN
    lanes = frames * N1

    def table_copy(j):
        at = pl.ds(j * height, height)
        return pltpu.make_async_copy(table_hbm.at[at], table.at[at], table_sem.at[j])

    def traces_copy(i, half):
        at = pl.ds((half * chunks + i) * width, width)
        return pltpu.make_async_copy(
            traces_hbm.at[:, at], traces.at[i, half], traces_sem.at[i, half]
        )

    def out_copy(i, j):
        at = (pl.ds(j * owners, owners), slice(None), pl.ds(i * lanes, lanes))
        return pltpu.make_async_copy(out.at[at], out_hbm.at[at], out_sem.at[i, j])

    traces_copy(0, 0).start()
    table_copy(0).start()
    traces_copy(0, 1).start()
    for j in range(1, parts):
        table_copy(j).start()
    for i in range(1, chunks):
        for half in range(2):
            traces_copy(i, half).start()
    for i in range(chunks):
        for half in range(2):
            traces_copy(i, half).wait()
        samples = jnp.concatenate(
            [
                traces[i, half, :, m * FLEN : (m + 1) * FLEN]
                for half in range(2)
                for m in range(frames)
            ],
            axis=0,
        )
        for j in range(parts):
            if i == 0:
                table_copy(j).wait()
            part = lax.dot_general(
                table[j * height : (j + 1) * height, :],
                samples,
                (((1,), (1,)), ((), ())),
                preferred_element_type=jnp.float32,
            )
            part = part.reshape(owners, rows, 2 * lanes)
            both = jnp.concatenate([part[:, :, :lanes], part[:, :, lanes:]], axis=1)
            out[j * owners : (j + 1) * owners, :, i * lanes : (i + 1) * lanes] = both.astype(
                jnp.bfloat16
            )
            out_copy(i, j).start()
    for i in range(chunks):
        for j in range(parts):
            out_copy(i, j).wait()


def sections_kernel(
    bins,
    cells_ref,
    first_ref,
    second_ref,
    third_ref,
    fourth_ref,
    forward_ref,
    inverse_ref,
    mask_ref,
    power_ref,
    cells,
    turned,
    kept,
    back,
    power_rows,
):
    rows = 4 * bins
    group = 16
    count = 4 * bins
    step = 2
    bf16 = jnp.bfloat16
    dot = functools.partial(jnp.dot, preferred_element_type=jnp.float32)
    for g in range(N2 // group):
        for m in range(2):
            block = cells_ref[g * group : (g + 1) * group, :, m * N1 : (m + 1) * N1]
            block = jnp.swapaxes(block, 0, 1)
            for r in range(rows):
                half, x, f = r // (2 * bins), r // bins % 2, r % bins
                n = (m * 2 + half) * bins + f
                cells[
                    x * N2 + g * group : x * N2 + (g + 1) * group, n * N1 : (n + 1) * N1
                ] = block[r]
    fwd_cos, fwd_sin = forward_ref[0], forward_ref[1]
    for n0 in range(0, count, step):
        summed = dot(first_ref[...], cells[:, n0 * N1 : (n0 + step) * N1])
        for i in range(step):
            n = n0 + i
            re = summed[:N2, i * N1 : (i + 1) * N1]
            im = summed[N2:, i * N1 : (i + 1) * N1]
            turned[n * N2 : (n + 1) * N2, :N1] = (re * fwd_cos - im * fwd_sin).astype(bf16)
            turned[n * N2 : (n + 1) * N2, N1:] = (re * fwd_sin + im * fwd_cos).astype(bf16)
    for n0 in range(0, count, step):
        section = dot(turned[n0 * N2 : (n0 + step) * N2, :], second_ref[...]).astype(bf16)
        for i in range(step):
            n = n0 + i
            mask = mask_ref[n % bins]
            for x in range(2):
                kept[n * N2 : (n + 1) * N2, x * N1 : (x + 1) * N1] = (
                    section[i * N2 : (i + 1) * N2, x * N1 : (x + 1) * N1] * mask
                )
    inv_cos, inv_sin = inverse_ref[0], inverse_ref[1]
    for n0 in range(0, count, step):
        summed = dot(kept[n0 * N2 : (n0 + step) * N2, :], third_ref[...])
        for i in range(step):
            n = n0 + i
            re = summed[i * N2 : (i + 1) * N2, :N1]
            im = summed[i * N2 : (i + 1) * N2, N1:]
            back[:N2, n * N1 : (n + 1) * N1] = (re * inv_cos - im * inv_sin).astype(bf16)
            back[N2:, n * N1 : (n + 1) * N1] = (re * inv_sin + im * inv_cos).astype(bf16)
    for n0 in range(0, count, step):
        filtered = dot(fourth_ref[...], back[:, n0 * N1 : (n0 + step) * N1])
        filtered = filtered.astype(bf16).astype(jnp.float32)
        power = filtered[:N2] * filtered[:N2] + filtered[N2:] * filtered[N2:]
        for i in range(step):
            power_rows[n0 + i] = power[:, i * N1 : (i + 1) * N1].astype(bf16)
    power_ref[...] = jnp.swapaxes(power_rows[...], 0, 1)


def cepstra_kernel(power_ref, weights_ref, cosine_ref, out_ref):
    sources, rows, lanes = power_ref.shape
    power = power_ref[...].reshape(sources * rows, lanes)
    energy = jnp.dot(weights_ref[...], power, preferred_element_type=jnp.float32)
    logs = jnp.log(jnp.maximum(energy, energy_floor))
    for k in range(4):
        cepstra = jnp.dot(
            cosine_ref[...],
            logs[k * NB : (k + 1) * NB],
            precision=lax.Precision.HIGHEST,
            preferred_element_type=jnp.float32,
        )
        m, half = k // 2, k % 2
        for i in range(lanes // N1):
            out_ref[half, 2 * i + m] = cepstra[:, i * N1 : (i + 1) * N1]


def whole(shape):
    return pl.BlockSpec(shape, lambda i: (0,) * len(shape))


VMEM_LIMIT = 48 * 1024 * 1024


def shards(traces, fan_mask, band_edges):
    axes = ("chan", "sub")
    devices = lax.axis_size("chan") * lax.axis_size("sub")
    sub_count = lax.axis_size("sub")
    bins = NF // devices
    rows = 4 * bins
    bf16 = jnp.bfloat16
    params = pltpu.CompilerParams(vmem_limit_bytes=VMEM_LIMIT)

    chunks, parts = 2, 2
    spectrum = pl.pallas_call(
        functools.partial(spectrum_kernel, devices, chunks, parts),
        in_specs=[pl.BlockSpec(memory_space=pltpu.HBM)] * 2,
        out_specs=pl.BlockSpec(memory_space=pltpu.HBM),
        out_shape=jax.ShapeDtypeStruct((devices, rows, HALF * N1), bf16),
        scratch_shapes=[
            pltpu.VMEM((2 * NF, FLEN), bf16),
            pltpu.VMEM((chunks, 2, N1, HALF // chunks * FLEN), bf16),
            pltpu.VMEM((devices, rows, HALF * N1), bf16),
            pltpu.SemaphoreType.DMA((parts,)),
            pltpu.SemaphoreType.DMA((chunks, 2)),
            pltpu.SemaphoreType.DMA((chunks, parts)),
        ],
        compiler_params=params,
        name="spectrum",
    )(jnp.asarray(time_table(devices)), traces)

    cells = lax.all_to_all(spectrum, axes, split_axis=0, concat_axis=0, tiled=True)

    mask = lax.dynamic_slice_in_dim(fan_mask, lax.axis_index("sub") * bins, bins, 0)
    mask = jnp.transpose(mask.reshape(bins, N1, N2), (0, 2, 1))
    mask = (mask > 0).astype(bf16)

    power = pl.pallas_call(
        functools.partial(sections_kernel, bins),
        grid=(HALF // 2,),
        in_specs=[
            pl.BlockSpec((N2, rows, 2 * N1), lambda i: (0, 0, i)),
            whole((2 * N2, 2 * N2)),
            whole((2 * N1, 2 * N1)),
            whole((2 * N1, 2 * N1)),
            whole((2 * N2, 2 * N2)),
            whole((2, N2, N1)),
            whole((2, N2, N1)),
            whole((bins, N2, N1)),
        ],
        out_specs=pl.BlockSpec((N2, rows, N1), lambda i: (0, 0, i)),
        out_shape=jax.ShapeDtypeStruct((N2, rows, HALF // 2 * N1), bf16),
        scratch_shapes=[
            pltpu.VMEM((2 * N2, rows * N1), bf16),
            pltpu.VMEM((rows * N2, 2 * N1), bf16),
            pltpu.VMEM((rows * N2, 2 * N1), bf16),
            pltpu.VMEM((2 * N2, rows * N1), bf16),
            pltpu.VMEM((rows, N2, N1), bf16),
        ],
        compiler_params=params,
        name="sections",
    )(
        cells,
        jnp.asarray(left_table(N2, -1.0)),
        jnp.asarray(right_table(N1, -1.0)),
        jnp.asarray(right_table(N1, 1.0)),
        jnp.asarray(left_table(N2, 1.0)),
        jnp.asarray(twiddle(-1.0)),
        jnp.asarray(twiddle(1.0)),
        mask,
    )

    returned = lax.all_to_all(power, axes, split_axis=0, concat_axis=0, tiled=True)

    weights = band_weights(band_edges).reshape(1, NB, devices, 1, bins)
    same = jnp.eye(4, dtype=bool)[:, None, None, :, None]
    weights = jnp.where(same, weights, jnp.zeros((), bf16)).reshape(4 * NB, devices * rows)
    cepstra = pl.pallas_call(
        cepstra_kernel,
        in_specs=[pl.BlockSpec(memory_space=pltpu.VMEM)] * 3,
        out_specs=pl.BlockSpec(memory_space=pltpu.VMEM),
        out_shape=jax.ShapeDtypeStruct((2, HALF, NB, N1), jnp.float32),
        compiler_params=params,
        name="cepstra",
    )(returned, weights, jnp.asarray(cosine_table()))
    return cepstra.reshape(FRAMES, NB, N1)


def solution(mesh):
    in_specs = (P(("chan", "sub"), None), P("chan", None), P())
    out_specs = P(None, None, ("chan", "sub"))
    return jax.shard_map(shards, mesh=mesh, in_specs=in_specs, out_specs=out_specs, check_vma=False)
```

```python
import functools
import math

import jax
import jax.numpy as jnp
import ml_dtypes
import numpy as np
from jax import lax
from jax.experimental import pallas as pl
from jax.experimental.pallas import tpu as pltpu
from jax.sharding import PartitionSpec as P

NCH = 16384
N1 = 128
N2 = 128
FLEN = 1024
NF = 512
NB = 64
FRAMES = 16
HALF = FRAMES // 2

energy_floor = 0.05


def time_table(devices):
    bins = NF // devices
    t = np.arange(FLEN)
    f = np.arange(NF)
    hann = 0.5 - 0.5 * np.cos(2.0 * math.pi * t / FLEN)
    phases = 2.0 * math.pi / FLEN * ((f[:, None] * t[None, :]) % FLEN)
    factor = (0.375 * FLEN) ** -0.5
    table = np.stack([np.cos(phases), -np.sin(phases)], axis=0) * (hann * factor)
    table = table.reshape(2, devices, bins, FLEN).transpose(1, 0, 2, 3)
    return table.reshape(2 * NF, FLEN).astype(ml_dtypes.bfloat16)


def dft_parts(length, sign):
    n = np.arange(length)
    phases = 2.0 * math.pi / length * ((n[:, None] * n[None, :]) % length)
    factor = length**-0.5
    return np.cos(phases) * factor, sign * np.sin(phases) * factor


def left_table(length, sign):
    re, im = dft_parts(length, sign)
    return np.block([[re, -im], [im, re]]).astype(ml_dtypes.bfloat16)


def right_table(length, sign):
    re, im = dft_parts(length, sign)
    return np.block([[re, im], [-im, re]]).astype(ml_dtypes.bfloat16)


def twiddle(sign):
    q = np.arange(N2)
    a = np.arange(N1)
    phases = 2.0 * math.pi / NCH * ((q[:, None] * a[None, :]) % NCH)
    return np.stack([np.cos(phases), sign * np.sin(phases)]).astype(np.float32)


def cosine_table():
    j = np.arange(NB)
    phases = math.pi / (2 * NB) * ((j[:, None] * (2 * j[None, :] + 1)) % (4 * NB))
    weight = np.where(j == 0, (1.0 / NB) ** 0.5, (2.0 / NB) ** 0.5)
    return (np.cos(phases) * weight[:, None]).astype(np.float32)


def band_weights(band_edges):
    bounds = band_edges.astype(jnp.float32)
    freq = jnp.arange(NF, dtype=jnp.int32).astype(jnp.float32)[None, :]
    low, middle, high = bounds[:-2, None], bounds[1:-1, None], bounds[2:, None]
    rising = (freq - low) / (middle - low)
    falling = (high - freq) / (high - middle)
    return jnp.maximum(jnp.minimum(rising, falling), 0.0).astype(jnp.bfloat16)


def spectrum_kernel(
    devices,
    chunks,
    parts,
    table_hbm,
    traces_hbm,
    out_hbm,
    table,
    traces,
    out,
    table_sem,
    traces_sem,
    out_sem,
):
    rows = 2 * NF // devices
    height = 2 * NF // parts
    owners = devices // parts
    frames = HALF // chunks
    width = frames * FLEN
    lanes = frames * N1

    def table_copy(j):
        at = pl.ds(j * height, height)
        return pltpu.make_async_copy(table_hbm.at[at], table.at[at], table_sem.at[j])

    def traces_copy(i, half):
        at = pl.ds((half * chunks + i) * width, width)
        return pltpu.make_async_copy(
            traces_hbm.at[:, at], traces.at[i, half], traces_sem.at[i, half]
        )

    def out_copy(i, j):
        at = (pl.ds(j * owners, owners), slice(None), pl.ds(i * lanes, lanes))
        return pltpu.make_async_copy(out.at[at], out_hbm.at[at], out_sem.at[i, j])

    traces_copy(0, 0).start()
    table_copy(0).start()
    traces_copy(0, 1).start()
    for j in range(1, parts):
        table_copy(j).start()
    for i in range(1, chunks):
        for half in range(2):
            traces_copy(i, half).start()
    for i in range(chunks):
        for half in range(2):
            traces_copy(i, half).wait()
        samples = jnp.concatenate(
            [
                traces[i, half, :, m * FLEN : (m + 1) * FLEN]
                for half in range(2)
                for m in range(frames)
            ],
            axis=0,
        )
        for j in range(parts):
            if i == 0:
                table_copy(j).wait()
            part = lax.dot_general(
                table[j * height : (j + 1) * height, :],
                samples,
                (((1,), (1,)), ((), ())),
                preferred_element_type=jnp.float32,
            )
            part = part.reshape(owners, rows, 2 * lanes)
            both = jnp.concatenate([part[:, :, :lanes], part[:, :, lanes:]], axis=1)
            out[j * owners : (j + 1) * owners, :, i * lanes : (i + 1) * lanes] = both.astype(
                jnp.bfloat16
            )
            out_copy(i, j).start()
    for i in range(chunks):
        for j in range(parts):
            out_copy(i, j).wait()


def sections_kernel(
    bins,
    cells_ref,
    first_ref,
    second_ref,
    third_ref,
    fourth_ref,
    forward_ref,
    inverse_ref,
    mask_ref,
    power_ref,
    cells,
    turned,
    kept,
    back,
    power_rows,
):
    rows = 4 * bins
    group = 16
    count = 4 * bins
    step = 2
    bf16 = jnp.bfloat16
    dot = functools.partial(jnp.dot, preferred_element_type=jnp.float32)
    for g in range(N2 // group):
        for m in range(2):
            block = cells_ref[g * group : (g + 1) * group, :, m * N1 : (m + 1) * N1]
            block = jnp.swapaxes(block, 0, 1)
            for r in range(rows):
                half, x, f = r // (2 * bins), r // bins % 2, r % bins
                n = (m * 2 + half) * bins + f
                cells[
                    x * N2 + g * group : x * N2 + (g + 1) * group, n * N1 : (n + 1) * N1
                ] = block[r]
    fwd_cos, fwd_sin = forward_ref[0], forward_ref[1]
    for n0 in range(0, count, step):
        summed = dot(first_ref[...], cells[:, n0 * N1 : (n0 + step) * N1])
        for i in range(step):
            n = n0 + i
            re = summed[:N2, i * N1 : (i + 1) * N1]
            im = summed[N2:, i * N1 : (i + 1) * N1]
            turned[n * N2 : (n + 1) * N2, :N1] = (re * fwd_cos - im * fwd_sin).astype(bf16)
            turned[n * N2 : (n + 1) * N2, N1:] = (re * fwd_sin + im * fwd_cos).astype(bf16)
    for n0 in range(0, count, step):
        section = dot(turned[n0 * N2 : (n0 + step) * N2, :], second_ref[...]).astype(bf16)
        for i in range(step):
            n = n0 + i
            mask = mask_ref[n % bins]
            for x in range(2):
                kept[n * N2 : (n + 1) * N2, x * N1 : (x + 1) * N1] = (
                    section[i * N2 : (i + 1) * N2, x * N1 : (x + 1) * N1] * mask
                )
    inv_cos, inv_sin = inverse_ref[0], inverse_ref[1]
    for n0 in range(0, count, step):
        summed = dot(kept[n0 * N2 : (n0 + step) * N2, :], third_ref[...])
        for i in range(step):
            n = n0 + i
            re = summed[i * N2 : (i + 1) * N2, :N1]
            im = summed[i * N2 : (i + 1) * N2, N1:]
            back[:N2, n * N1 : (n + 1) * N1] = (re * inv_cos - im * inv_sin).astype(bf16)
            back[N2:, n * N1 : (n + 1) * N1] = (re * inv_sin + im * inv_cos).astype(bf16)
    for n0 in range(0, count, step):
        filtered = dot(fourth_ref[...], back[:, n0 * N1 : (n0 + step) * N1])
        filtered = filtered.astype(bf16).astype(jnp.float32)
        power = filtered[:N2] * filtered[:N2] + filtered[N2:] * filtered[N2:]
        for i in range(step):
            power_rows[n0 + i] = power[:, i * N1 : (i + 1) * N1].astype(bf16)
    power_ref[...] = jnp.swapaxes(power_rows[...], 0, 1)


def cepstra_kernel(power_ref, weights_ref, cosine_ref, out_ref):
    sources, rows, lanes = power_ref.shape
    power = power_ref[...].reshape(sources * rows, lanes)
    energy = jnp.dot(weights_ref[...], power, preferred_element_type=jnp.float32)
    logs = jnp.log(jnp.maximum(energy, energy_floor))
    for k in range(4):
        cepstra = jnp.dot(
            cosine_ref[...],
            logs[k * NB : (k + 1) * NB],
            precision=lax.Precision.HIGHEST,
            preferred_element_type=jnp.float32,
        )
        m, half = k // 2, k % 2
        for i in range(lanes // N1):
            out_ref[half, 2 * i + m] = cepstra[:, i * N1 : (i + 1) * N1]


def whole(shape):
    return pl.BlockSpec(shape, lambda i: (0,) * len(shape))


VMEM_LIMIT = 48 * 1024 * 1024
VMEM_WHOLE = 60 * 1024 * 1024


def shards(traces, fan_mask, band_edges):
    axes = ("chan", "sub")
    devices = lax.axis_size("chan") * lax.axis_size("sub")
    sub_count = lax.axis_size("sub")
    bins = NF // devices
    rows = 4 * bins
    bf16 = jnp.bfloat16
    params = pltpu.CompilerParams(vmem_limit_bytes=VMEM_LIMIT)

    chunks, parts = 2, 2
    spectrum = pl.pallas_call(
        functools.partial(spectrum_kernel, devices, chunks, parts),
        in_specs=[pl.BlockSpec(memory_space=pltpu.HBM)] * 2,
        out_specs=pl.BlockSpec(memory_space=pltpu.HBM),
        out_shape=jax.ShapeDtypeStruct((devices, rows, HALF * N1), bf16),
        scratch_shapes=[
            pltpu.VMEM((2 * NF, FLEN), bf16),
            pltpu.VMEM((chunks, 2, N1, HALF // chunks * FLEN), bf16),
            pltpu.VMEM((devices, rows, HALF * N1), bf16),
            pltpu.SemaphoreType.DMA((parts,)),
            pltpu.SemaphoreType.DMA((chunks, 2)),
            pltpu.SemaphoreType.DMA((chunks, parts)),
        ],
        compiler_params=pltpu.CompilerParams(vmem_limit_bytes=VMEM_WHOLE),
        name="spectrum",
    )(jnp.asarray(time_table(devices)), traces)

    cells = lax.all_to_all(spectrum, axes, split_axis=0, concat_axis=0, tiled=True)

    mask = lax.dynamic_slice_in_dim(fan_mask, lax.axis_index("sub") * bins, bins, 0)
    mask = jnp.transpose(mask.reshape(bins, N1, N2), (0, 2, 1))
    mask = (mask > 0).astype(bf16)

    power = pl.pallas_call(
        functools.partial(sections_kernel, bins),
        grid=(HALF // 2,),
        in_specs=[
            pl.BlockSpec((N2, rows, 2 * N1), lambda i: (0, 0, i)),
            whole((2 * N2, 2 * N2)),
            whole((2 * N1, 2 * N1)),
            whole((2 * N1, 2 * N1)),
            whole((2 * N2, 2 * N2)),
            whole((2, N2, N1)),
            whole((2, N2, N1)),
            whole((bins, N2, N1)),
        ],
        out_specs=pl.BlockSpec((N2, rows, N1), lambda i: (0, 0, i)),
        out_shape=jax.ShapeDtypeStruct((N2, rows, HALF // 2 * N1), bf16),
        scratch_shapes=[
            pltpu.VMEM((2 * N2, rows * N1), bf16),
            pltpu.VMEM((rows * N2, 2 * N1), bf16),
            pltpu.VMEM((rows * N2, 2 * N1), bf16),
            pltpu.VMEM((2 * N2, rows * N1), bf16),
            pltpu.VMEM((rows, N2, N1), bf16),
        ],
        compiler_params=params,
        name="sections",
    )(
        cells,
        jnp.asarray(left_table(N2, -1.0)),
        jnp.asarray(right_table(N1, -1.0)),
        jnp.asarray(right_table(N1, 1.0)),
        jnp.asarray(left_table(N2, 1.0)),
        jnp.asarray(twiddle(-1.0)),
        jnp.asarray(twiddle(1.0)),
        mask,
    )

    returned = lax.all_to_all(power, axes, split_axis=0, concat_axis=0, tiled=True)

    weights = band_weights(band_edges).reshape(1, NB, devices, 1, bins)
    same = jnp.eye(4, dtype=bool)[:, None, None, :, None]
    weights = jnp.where(same, weights, jnp.zeros((), bf16)).reshape(4 * NB, devices * rows)
    cepstra = pl.pallas_call(
        cepstra_kernel,
        in_specs=[pl.BlockSpec(memory_space=pltpu.VMEM)] * 3,
        out_specs=pl.BlockSpec(memory_space=pltpu.VMEM),
        out_shape=jax.ShapeDtypeStruct((2, HALF, NB, N1), jnp.float32),
        compiler_params=params,
        name="cepstra",
    )(returned, weights, jnp.asarray(cosine_table()))
    return cepstra.reshape(FRAMES, NB, N1)


def solution(mesh):
    in_specs = (P(("chan", "sub"), None), P("chan", None), P())
    out_specs = P(None, None, ("chan", "sub"))
    return jax.shard_map(shards, mesh=mesh, in_specs=in_specs, out_specs=out_specs, check_vma=False)
```

```python
import functools
import math

import jax
import jax.numpy as jnp
import ml_dtypes
import numpy as np
from jax import lax
from jax.experimental import pallas as pl
from jax.experimental.pallas import tpu as pltpu
from jax.sharding import PartitionSpec as P

NCH = 16384
N1 = 128
N2 = 128
FLEN = 1024
NF = 512
NB = 64
FRAMES = 16
HALF = FRAMES // 2
PIECES = 2

energy_floor = 0.05


def time_table(devices):
    bins = NF // devices
    t = np.arange(FLEN)
    f = np.arange(NF)
    hann = 0.5 - 0.5 * np.cos(2.0 * math.pi * t / FLEN)
    phases = 2.0 * math.pi / FLEN * ((f[:, None] * t[None, :]) % FLEN)
    factor = (0.375 * FLEN) ** -0.5
    table = np.stack([np.cos(phases), -np.sin(phases)], axis=0) * (hann * factor)
    table = table.reshape(2, devices, bins, FLEN).transpose(1, 0, 2, 3)
    return table.reshape(2 * NF, FLEN).astype(ml_dtypes.bfloat16)


def dft_parts(length, sign):
    n = np.arange(length)
    phases = 2.0 * math.pi / length * ((n[:, None] * n[None, :]) % length)
    factor = length**-0.5
    return np.cos(phases) * factor, sign * np.sin(phases) * factor


def left_table(length, sign):
    re, im = dft_parts(length, sign)
    return np.block([[re, -im], [im, re]]).astype(ml_dtypes.bfloat16)


def right_table(length, sign):
    re, im = dft_parts(length, sign)
    return np.block([[re, im], [-im, re]]).astype(ml_dtypes.bfloat16)


def twiddle(sign):
    q = np.arange(N2)
    a = np.arange(N1)
    phases = 2.0 * math.pi / NCH * ((q[:, None] * a[None, :]) % NCH)
    return np.stack([np.cos(phases), sign * np.sin(phases)]).astype(np.float32)


def cosine_table():
    j = np.arange(NB)
    phases = math.pi / (2 * NB) * ((j[:, None] * (2 * j[None, :] + 1)) % (4 * NB))
    weight = np.where(j == 0, (1.0 / NB) ** 0.5, (2.0 / NB) ** 0.5)
    return (np.cos(phases) * weight[:, None]).astype(np.float32)


def band_weights(band_edges):
    bounds = band_edges.astype(jnp.float32)
    freq = jnp.arange(NF, dtype=jnp.int32).astype(jnp.float32)[None, :]
    low, middle, high = bounds[:-2, None], bounds[1:-1, None], bounds[2:, None]
    rising = (freq - low) / (middle - low)
    falling = (high - freq) / (high - middle)
    return jnp.maximum(jnp.minimum(rising, falling), 0.0).astype(jnp.bfloat16)


def spectrum_kernel(
    devices,
    piece,
    chunks,
    parts,
    table_hbm,
    traces_hbm,
    out_hbm,
    table,
    traces,
    out,
    table_sem,
    traces_sem,
    out_sem,
):
    rows = 2 * NF // devices
    height = 2 * NF // parts
    owners = devices // parts
    frames = HALF // PIECES // chunks
    width = frames * FLEN
    lanes = frames * N1

    def table_copy(j):
        at = pl.ds(j * height, height)
        return pltpu.make_async_copy(table_hbm.at[at], table.at[at], table_sem.at[j])

    def traces_copy(i, half):
        at = pl.ds(((half * PIECES + piece) * chunks + i) * width, width)
        return pltpu.make_async_copy(
            traces_hbm.at[:, at], traces.at[i, half], traces_sem.at[i, half]
        )

    def out_copy(i, j):
        at = (pl.ds(j * owners, owners), slice(None), pl.ds(i * lanes, lanes))
        return pltpu.make_async_copy(out.at[at], out_hbm.at[at], out_sem.at[i, j])

    traces_copy(0, 0).start()
    table_copy(0).start()
    traces_copy(0, 1).start()
    for j in range(1, parts):
        table_copy(j).start()
    for i in range(1, chunks):
        for half in range(2):
            traces_copy(i, half).start()
    for i in range(chunks):
        for half in range(2):
            traces_copy(i, half).wait()
        samples = jnp.concatenate(
            [
                traces[i, half, :, m * FLEN : (m + 1) * FLEN]
                for half in range(2)
                for m in range(frames)
            ],
            axis=0,
        )
        for j in range(parts):
            if i == 0:
                table_copy(j).wait()
            part = lax.dot_general(
                table[j * height : (j + 1) * height, :],
                samples,
                (((1,), (1,)), ((), ())),
                preferred_element_type=jnp.float32,
            )
            part = part.reshape(owners, rows, 2 * lanes)
            both = jnp.concatenate([part[:, :, :lanes], part[:, :, lanes:]], axis=1)
            out[j * owners : (j + 1) * owners, :, i * lanes : (i + 1) * lanes] = both.astype(
                jnp.bfloat16
            )
            out_copy(i, j).start()
    for i in range(chunks):
        for j in range(parts):
            out_copy(i, j).wait()


def sections_kernel(
    bins,
    earlier,
    cells_ref,
    first_ref,
    second_ref,
    third_ref,
    fourth_ref,
    forward_ref,
    inverse_ref,
    mask_ref,
    *refs,
):
    power_ref, cells, turned, kept, back, power_rows = refs[earlier:]
    rows = 4 * bins
    group = 16
    count = 4 * bins
    step = 2
    bf16 = jnp.bfloat16
    dot = functools.partial(jnp.dot, preferred_element_type=jnp.float32)
    for g in range(N2 // group):
        for m in range(2):
            block = cells_ref[g * group : (g + 1) * group, :, m * N1 : (m + 1) * N1]
            block = jnp.swapaxes(block, 0, 1)
            for r in range(rows):
                half, x, f = r // (2 * bins), r // bins % 2, r % bins
                n = (m * 2 + half) * bins + f
                cells[
                    x * N2 + g * group : x * N2 + (g + 1) * group, n * N1 : (n + 1) * N1
                ] = block[r]
    fwd_cos, fwd_sin = forward_ref[0], forward_ref[1]
    for n0 in range(0, count, step):
        summed = dot(first_ref[...], cells[:, n0 * N1 : (n0 + step) * N1])
        for i in range(step):
            n = n0 + i
            re = summed[:N2, i * N1 : (i + 1) * N1]
            im = summed[N2:, i * N1 : (i + 1) * N1]
            turned[n * N2 : (n + 1) * N2, :N1] = (re * fwd_cos - im * fwd_sin).astype(bf16)
            turned[n * N2 : (n + 1) * N2, N1:] = (re * fwd_sin + im * fwd_cos).astype(bf16)
    for n0 in range(0, count, step):
        section = dot(turned[n0 * N2 : (n0 + step) * N2, :], second_ref[...]).astype(bf16)
        for i in range(step):
            n = n0 + i
            mask = mask_ref[n % bins]
            for x in range(2):
                kept[n * N2 : (n + 1) * N2, x * N1 : (x + 1) * N1] = (
                    section[i * N2 : (i + 1) * N2, x * N1 : (x + 1) * N1] * mask
                )
    inv_cos, inv_sin = inverse_ref[0], inverse_ref[1]
    for n0 in range(0, count, step):
        summed = dot(kept[n0 * N2 : (n0 + step) * N2, :], third_ref[...])
        for i in range(step):
            n = n0 + i
            re = summed[i * N2 : (i + 1) * N2, :N1]
            im = summed[i * N2 : (i + 1) * N2, N1:]
            back[:N2, n * N1 : (n + 1) * N1] = (re * inv_cos - im * inv_sin).astype(bf16)
            back[N2:, n * N1 : (n + 1) * N1] = (re * inv_sin + im * inv_cos).astype(bf16)
    for n0 in range(0, count, step):
        filtered = dot(fourth_ref[...], back[:, n0 * N1 : (n0 + step) * N1])
        filtered = filtered.astype(bf16).astype(jnp.float32)
        power = filtered[:N2] * filtered[:N2] + filtered[N2:] * filtered[N2:]
        for i in range(step):
            power_rows[n0 + i] = power[:, i * N1 : (i + 1) * N1].astype(bf16)
    power_ref[...] = jnp.swapaxes(power_rows[...], 0, 1)


def cepstra_kernel(power_ref, weights_ref, cosine_ref, out_ref):
    sources, rows, lanes = power_ref.shape
    power = power_ref[...].reshape(sources * rows, lanes)
    energy = jnp.dot(weights_ref[...], power, preferred_element_type=jnp.float32)
    logs = jnp.log(jnp.maximum(energy, energy_floor))
    for k in range(4):
        cepstra = jnp.dot(
            cosine_ref[...],
            logs[k * NB : (k + 1) * NB],
            precision=lax.Precision.HIGHEST,
            preferred_element_type=jnp.float32,
        )
        m, half = k // 2, k % 2
        for i in range(lanes // N1):
            out_ref[half, 2 * i + m] = cepstra[:, i * N1 : (i + 1) * N1]


def whole(shape):
    return pl.BlockSpec(shape, lambda i: (0,) * len(shape))


VMEM_LIMIT = 48 * 1024 * 1024
VMEM_WHOLE = 60 * 1024 * 1024


def shards(traces, fan_mask, band_edges):
    axes = ("chan", "sub")
    devices = lax.axis_size("chan") * lax.axis_size("sub")
    sub_count = lax.axis_size("sub")
    bins = NF // devices
    rows = 4 * bins
    bf16 = jnp.bfloat16
    params = pltpu.CompilerParams(vmem_limit_bytes=VMEM_LIMIT)

    chunks, parts = 2, 2
    lanes = HALF // PIECES * N1
    table = jnp.asarray(time_table(devices))
    cells = []
    for piece in range(PIECES):
        spectrum = pl.pallas_call(
            functools.partial(spectrum_kernel, devices, piece, chunks, parts),
            in_specs=[pl.BlockSpec(memory_space=pltpu.HBM)] * 2,
            out_specs=pl.BlockSpec(memory_space=pltpu.HBM),
            out_shape=jax.ShapeDtypeStruct((devices, rows, lanes), bf16),
            scratch_shapes=[
                pltpu.VMEM((2 * NF, FLEN), bf16),
                pltpu.VMEM((chunks, 2, N1, HALF // PIECES // chunks * FLEN), bf16),
                pltpu.VMEM((devices, rows, lanes), bf16),
                pltpu.SemaphoreType.DMA((parts,)),
                pltpu.SemaphoreType.DMA((chunks, 2)),
                pltpu.SemaphoreType.DMA((chunks, parts)),
            ],
            compiler_params=pltpu.CompilerParams(vmem_limit_bytes=VMEM_WHOLE),
            cost_estimate=pl.CostEstimate(
                flops=4 * NF * FLEN * N1 * FRAMES // PIECES,
                bytes_accessed=6 * 1024 * 1024,
                transcendentals=0,
            ),
            name="spectrum",
        )(table, traces)
        cells.append(
            lax.all_to_all(spectrum, axes, split_axis=0, concat_axis=0, tiled=True)
        )

    mask = lax.dynamic_slice_in_dim(fan_mask, lax.axis_index("sub") * bins, bins, 0)
    mask = jnp.transpose(mask.reshape(bins, N1, N2), (0, 2, 1))
    mask = (mask > 0).astype(bf16)

    tables = (
        jnp.asarray(left_table(N2, -1.0)),
        jnp.asarray(right_table(N1, -1.0)),
        jnp.asarray(right_table(N1, 1.0)),
        jnp.asarray(left_table(N2, 1.0)),
        jnp.asarray(twiddle(-1.0)),
        jnp.asarray(twiddle(1.0)),
        mask,
    )
    steps = HALF // 2 // PIECES
    power = None
    for piece in range(PIECES):
        earlier = () if power is None else (power,)
        power = pl.pallas_call(
            functools.partial(sections_kernel, bins, len(earlier)),
            grid=(steps,),
            in_specs=[
                pl.BlockSpec((N2, rows, 2 * N1), lambda i: (0, 0, i)),
                whole((2 * N2, 2 * N2)),
                whole((2 * N1, 2 * N1)),
                whole((2 * N1, 2 * N1)),
                whole((2 * N2, 2 * N2)),
                whole((2, N2, N1)),
                whole((2, N2, N1)),
                whole((bins, N2, N1)),
            ]
            + [pl.BlockSpec(memory_space=pltpu.HBM)] * len(earlier),
            out_specs=pl.BlockSpec((N2, rows, N1), lambda i, at=piece * steps: (0, 0, i + at)),
            out_shape=jax.ShapeDtypeStruct((N2, rows, HALF // 2 * N1), bf16),
            scratch_shapes=[
                pltpu.VMEM((2 * N2, rows * N1), bf16),
                pltpu.VMEM((rows * N2, 2 * N1), bf16),
                pltpu.VMEM((rows * N2, 2 * N1), bf16),
                pltpu.VMEM((2 * N2, rows * N1), bf16),
                pltpu.VMEM((rows, N2, N1), bf16),
            ],
            input_output_aliases={8: 0} if earlier else {},
            compiler_params=params,
            cost_estimate=pl.CostEstimate(
                flops=4 * 2 * 4 * N1 * N1 * N1 * bins * FRAMES // PIECES,
                bytes_accessed=3 * 1024 * 1024,
                transcendentals=0,
            ),
            name="sections",
        )(cells[piece], *tables, *earlier)

    returned = lax.all_to_all(power, axes, split_axis=0, concat_axis=0, tiled=True)

    weights = band_weights(band_edges).reshape(1, NB, devices, 1, bins)
    same = jnp.eye(4, dtype=bool)[:, None, None, :, None]
    weights = jnp.where(same, weights, jnp.zeros((), bf16)).reshape(4 * NB, devices * rows)
    cepstra = pl.pallas_call(
        cepstra_kernel,
        in_specs=[pl.BlockSpec(memory_space=pltpu.VMEM)] * 3,
        out_specs=pl.BlockSpec(memory_space=pltpu.VMEM),
        out_shape=jax.ShapeDtypeStruct((2, HALF, NB, N1), jnp.float32),
        compiler_params=params,
        name="cepstra",
    )(returned, weights, jnp.asarray(cosine_table()))
    return cepstra.reshape(FRAMES, NB, N1)


def solution(mesh):
    in_specs = (P(("chan", "sub"), None), P("chan", None), P())
    out_specs = P(None, None, ("chan", "sub"))
    return jax.shard_map(shards, mesh=mesh, in_specs=in_specs, out_specs=out_specs, check_vma=False)
```

```python
import functools
import math

import jax
import jax.numpy as jnp
import ml_dtypes
import numpy as np
from jax import lax
from jax.experimental import pallas as pl
from jax.experimental.pallas import tpu as pltpu
from jax.sharding import Mesh
from jax.sharding import PartitionSpec as P

NCH = 16384
N1 = 128
N2 = 128
FLEN = 1024
NF = 512
NB = 64
FRAMES = 16
HALF = FRAMES // 2

energy_floor = 0.05

PLACES = {"x": 4, "zl": 2, "y": 4, "zh": 2, "core": 2}
ORDER = ("zl", "y", "core", "x", "zh")


def listed():
    names = tuple(PLACES)
    devices = np.arange(math.prod(PLACES.values())).reshape(tuple(PLACES.values()))
    return devices.transpose([names.index(name) for name in ORDER]).reshape(-1)


def time_table(devices):
    bins = NF // devices
    t = np.arange(FLEN)
    f = np.arange(NF)
    hann = 0.5 - 0.5 * np.cos(2.0 * math.pi * t / FLEN)
    phases = 2.0 * math.pi / FLEN * ((f[:, None] * t[None, :]) % FLEN)
    factor = (0.375 * FLEN) ** -0.5
    table = np.stack([np.cos(phases), -np.sin(phases)], axis=0) * (hann * factor)
    table = table.reshape(2, devices, bins, FLEN)[:, listed()].transpose(1, 0, 2, 3)
    return table.reshape(2 * NF, FLEN).astype(ml_dtypes.bfloat16)


def dft_parts(length, sign):
    n = np.arange(length)
    phases = 2.0 * math.pi / length * ((n[:, None] * n[None, :]) % length)
    factor = length**-0.5
    return np.cos(phases) * factor, sign * np.sin(phases) * factor


def left_table(length, sign):
    re, im = dft_parts(length, sign)
    return np.block([[re, -im], [im, re]]).astype(ml_dtypes.bfloat16)


def right_table(length, sign):
    re, im = dft_parts(length, sign)
    return np.block([[re, im], [-im, re]]).astype(ml_dtypes.bfloat16)


def twiddle(sign):
    q = np.arange(N2)
    a = np.arange(N1)
    phases = 2.0 * math.pi / NCH * ((q[:, None] * a[None, :]) % NCH)
    return np.stack([np.cos(phases), sign * np.sin(phases)]).astype(np.float32)


def cosine_table():
    j = np.arange(NB)
    phases = math.pi / (2 * NB) * ((j[:, None] * (2 * j[None, :] + 1)) % (4 * NB))
    weight = np.where(j == 0, (1.0 / NB) ** 0.5, (2.0 / NB) ** 0.5)
    return (np.cos(phases) * weight[:, None]).astype(np.float32)


def band_weights(band_edges, freq):
    bounds = band_edges.astype(jnp.float32)
    freq = freq.astype(jnp.float32)[None, :]
    low, middle, high = bounds[:-2, None], bounds[1:-1, None], bounds[2:, None]
    rising = (freq - low) / (middle - low)
    falling = (high - freq) / (high - middle)
    return jnp.maximum(jnp.minimum(rising, falling), 0.0).astype(jnp.bfloat16)


def spectrum_kernel(
    devices,
    chunks,
    parts,
    table_hbm,
    traces_hbm,
    out_hbm,
    table,
    traces,
    out,
    table_sem,
    traces_sem,
    out_sem,
):
    rows = 2 * NF // devices
    height = 2 * NF // parts
    owners = devices // parts
    frames = HALF // chunks
    width = frames * FLEN
    lanes = frames * N1

    def table_copy(j):
        at = pl.ds(j * height, height)
        return pltpu.make_async_copy(table_hbm.at[at], table.at[at], table_sem.at[j])

    def traces_copy(i, half):
        at = pl.ds((half * chunks + i) * width, width)
        return pltpu.make_async_copy(
            traces_hbm.at[:, at], traces.at[i, half], traces_sem.at[i, half]
        )

    def out_copy(i, j):
        at = (pl.ds(j * owners, owners), slice(None), pl.ds(i * lanes, lanes))
        return pltpu.make_async_copy(out.at[at], out_hbm.at[at], out_sem.at[i, j])

    traces_copy(0, 0).start()
    table_copy(0).start()
    traces_copy(0, 1).start()
    for j in range(1, parts):
        table_copy(j).start()
    for i in range(1, chunks):
        for half in range(2):
            traces_copy(i, half).start()
    for i in range(chunks):
        for half in range(2):
            traces_copy(i, half).wait()
        samples = jnp.concatenate(
            [
                traces[i, half, :, m * FLEN : (m + 1) * FLEN]
                for half in range(2)
                for m in range(frames)
            ],
            axis=0,
        )
        for j in range(parts):
            if i == 0:
                table_copy(j).wait()
            part = lax.dot_general(
                table[j * height : (j + 1) * height, :],
                samples,
                (((1,), (1,)), ((), ())),
                preferred_element_type=jnp.float32,
            )
            part = part.reshape(owners, rows, 2 * lanes)
            both = jnp.concatenate([part[:, :, :lanes], part[:, :, lanes:]], axis=1)
            out[j * owners : (j + 1) * owners, :, i * lanes : (i + 1) * lanes] = both.astype(
                jnp.bfloat16
            )
            out_copy(i, j).start()
    for i in range(chunks):
        for j in range(parts):
            out_copy(i, j).wait()


def sections_kernel(
    bins,
    cells_ref,
    first_ref,
    second_ref,
    third_ref,
    fourth_ref,
    forward_ref,
    inverse_ref,
    mask_ref,
    power_ref,
    cells,
    turned,
    kept,
    back,
    power_rows,
):
    rows = 4 * bins
    group = 16
    count = 4 * bins
    step = 2
    bf16 = jnp.bfloat16
    dot = functools.partial(jnp.dot, preferred_element_type=jnp.float32)
    for g in range(N2 // group):
        for m in range(2):
            block = cells_ref[g * group : (g + 1) * group, :, m * N1 : (m + 1) * N1]
            block = jnp.swapaxes(block, 0, 1)
            for r in range(rows):
                half, x, f = r // (2 * bins), r // bins % 2, r % bins
                n = (m * 2 + half) * bins + f
                cells[
                    x * N2 + g * group : x * N2 + (g + 1) * group, n * N1 : (n + 1) * N1
                ] = block[r]
    fwd_cos, fwd_sin = forward_ref[0], forward_ref[1]
    for n0 in range(0, count, step):
        summed = dot(first_ref[...], cells[:, n0 * N1 : (n0 + step) * N1])
        for i in range(step):
            n = n0 + i
            re = summed[:N2, i * N1 : (i + 1) * N1]
            im = summed[N2:, i * N1 : (i + 1) * N1]
            turned[n * N2 : (n + 1) * N2, :N1] = (re * fwd_cos - im * fwd_sin).astype(bf16)
            turned[n * N2 : (n + 1) * N2, N1:] = (re * fwd_sin + im * fwd_cos).astype(bf16)
    for n0 in range(0, count, step):
        section = dot(turned[n0 * N2 : (n0 + step) * N2, :], second_ref[...]).astype(bf16)
        for i in range(step):
            n = n0 + i
            mask = mask_ref[n % bins]
            for x in range(2):
                kept[n * N2 : (n + 1) * N2, x * N1 : (x + 1) * N1] = (
                    section[i * N2 : (i + 1) * N2, x * N1 : (x + 1) * N1] * mask
                )
    inv_cos, inv_sin = inverse_ref[0], inverse_ref[1]
    for n0 in range(0, count, step):
        summed = dot(kept[n0 * N2 : (n0 + step) * N2, :], third_ref[...])
        for i in range(step):
            n = n0 + i
            re = summed[i * N2 : (i + 1) * N2, :N1]
            im = summed[i * N2 : (i + 1) * N2, N1:]
            back[:N2, n * N1 : (n + 1) * N1] = (re * inv_cos - im * inv_sin).astype(bf16)
            back[N2:, n * N1 : (n + 1) * N1] = (re * inv_sin + im * inv_cos).astype(bf16)
    for n0 in range(0, count, step):
        filtered = dot(fourth_ref[...], back[:, n0 * N1 : (n0 + step) * N1])
        filtered = filtered.astype(bf16).astype(jnp.float32)
        power = filtered[:N2] * filtered[:N2] + filtered[N2:] * filtered[N2:]
        for i in range(step):
            power_rows[n0 + i] = power[:, i * N1 : (i + 1) * N1].astype(bf16)
    power_ref[...] = jnp.swapaxes(power_rows[...], 0, 1)


def cepstra_kernel(power_ref, weights_ref, cosine_ref, out_ref):
    sources, rows, lanes = power_ref.shape
    power = power_ref[...].reshape(sources * rows, lanes)
    energy = jnp.dot(weights_ref[...], power, preferred_element_type=jnp.float32)
    logs = jnp.log(jnp.maximum(energy, energy_floor))
    for k in range(4):
        cepstra = jnp.dot(
            cosine_ref[...],
            logs[k * NB : (k + 1) * NB],
            precision=lax.Precision.HIGHEST,
            preferred_element_type=jnp.float32,
        )
        m, half = k // 2, k % 2
        for i in range(lanes // N1):
            out_ref[half, 2 * i + m] = cepstra[:, i * N1 : (i + 1) * N1]


def whole(shape):
    return pl.BlockSpec(shape, lambda i: (0,) * len(shape))


VMEM_LIMIT = 48 * 1024 * 1024
VMEM_WHOLE = 60 * 1024 * 1024


def shards(traces, fan_mask, band_edges):
    devices = math.prod(lax.axis_size(name) for name in PLACES)
    bins = NF // devices
    order = np.concatenate([listed(), N2 + listed()])
    rows = 4 * bins
    bf16 = jnp.bfloat16
    params = pltpu.CompilerParams(vmem_limit_bytes=VMEM_LIMIT)

    chunks, parts = 2, 2
    spectrum = pl.pallas_call(
        functools.partial(spectrum_kernel, devices, chunks, parts),
        in_specs=[pl.BlockSpec(memory_space=pltpu.HBM)] * 2,
        out_specs=pl.BlockSpec(memory_space=pltpu.HBM),
        out_shape=jax.ShapeDtypeStruct((devices, rows, HALF * N1), bf16),
        scratch_shapes=[
            pltpu.VMEM((2 * NF, FLEN), bf16),
            pltpu.VMEM((chunks, 2, N1, HALF // chunks * FLEN), bf16),
            pltpu.VMEM((devices, rows, HALF * N1), bf16),
            pltpu.SemaphoreType.DMA((parts,)),
            pltpu.SemaphoreType.DMA((chunks, 2)),
            pltpu.SemaphoreType.DMA((chunks, parts)),
        ],
        compiler_params=pltpu.CompilerParams(vmem_limit_bytes=VMEM_WHOLE),
        name="spectrum",
    )(jnp.asarray(time_table(devices)), traces)

    cells = lax.all_to_all(spectrum, ORDER, split_axis=0, concat_axis=0, tiled=True)

    mask = lax.dynamic_slice_in_dim(fan_mask, lax.axis_index(("zh", "core")) * bins, bins, 0)
    mask = jnp.transpose(mask.reshape(bins, N1, N2), (0, 2, 1))
    mask = (mask > 0).astype(bf16)

    power = pl.pallas_call(
        functools.partial(sections_kernel, bins),
        grid=(HALF // 2,),
        in_specs=[
            pl.BlockSpec((N2, rows, 2 * N1), lambda i: (0, 0, i)),
            whole((2 * N2, 2 * N2)),
            whole((2 * N1, 2 * N1)),
            whole((2 * N1, 2 * N1)),
            whole((2 * N2, 2 * N2)),
            whole((2, N2, N1)),
            whole((2, N2, N1)),
            whole((bins, N2, N1)),
        ],
        out_specs=pl.BlockSpec((N2, rows, N1), lambda i: (0, 0, i)),
        out_shape=jax.ShapeDtypeStruct((N2, rows, HALF // 2 * N1), bf16),
        scratch_shapes=[
            pltpu.VMEM((2 * N2, rows * N1), bf16),
            pltpu.VMEM((rows * N2, 2 * N1), bf16),
            pltpu.VMEM((rows * N2, 2 * N1), bf16),
            pltpu.VMEM((2 * N2, rows * N1), bf16),
            pltpu.VMEM((rows, N2, N1), bf16),
        ],
        compiler_params=params,
        name="sections",
    )(
        cells,
        jnp.asarray(left_table(N2, -1.0)[:, order]),
        jnp.asarray(right_table(N1, -1.0)),
        jnp.asarray(right_table(N1, 1.0)),
        jnp.asarray(left_table(N2, 1.0)[order]),
        jnp.asarray(twiddle(-1.0)),
        jnp.asarray(twiddle(1.0)),
        mask,
    )

    returned = lax.all_to_all(power, ORDER, split_axis=0, concat_axis=0, tiled=True)

    freq = (listed()[:, None] * bins + np.arange(bins)).reshape(-1)
    weights = band_weights(band_edges, jnp.asarray(freq)).reshape(1, NB, devices, 1, bins)
    same = jnp.eye(4, dtype=bool)[:, None, None, :, None]
    weights = jnp.where(same, weights, jnp.zeros((), bf16)).reshape(4 * NB, devices * rows)
    cepstra = pl.pallas_call(
        cepstra_kernel,
        in_specs=[pl.BlockSpec(memory_space=pltpu.VMEM)] * 3,
        out_specs=pl.BlockSpec(memory_space=pltpu.VMEM),
        out_shape=jax.ShapeDtypeStruct((2, HALF, NB, N1), jnp.float32),
        compiler_params=params,
        name="cepstra",
    )(returned, weights, jnp.asarray(cosine_table()))
    return cepstra.reshape(FRAMES, NB, N1)


def solution(mesh):
    places = Mesh(mesh.devices.reshape(tuple(PLACES.values())), tuple(PLACES))
    whole_axes = tuple(PLACES)
    in_specs = (P(whole_axes, None), P(("x", "zl", "y"), None), P())
    out_specs = P(None, None, whole_axes)
    return jax.shard_map(
        shards, mesh=places, in_specs=in_specs, out_specs=out_specs, check_vma=False
    )
```

```python
import functools
import math

import jax
import jax.numpy as jnp
import ml_dtypes
import numpy as np
from jax import lax
from jax.experimental import pallas as pl
from jax.experimental.pallas import tpu as pltpu
from jax.sharding import Mesh
from jax.sharding import PartitionSpec as P

NCH = 16384
N1 = 128
N2 = 128
FLEN = 1024
NF = 512
NB = 64
FRAMES = 16
BLOCKS = 32
BINS = NF // BLOCKS
SHARES = 4
SHARE = FRAMES // SHARES
ROUND = 8
ROUNDS = -(-(BINS + 1) // ROUND)

energy_floor = 0.05

PLACES = {"x": 4, "zl": 2, "y": 4, "zh": 2, "core": 2}
ORDER = ("zl", "y", "core", "x", "zh")


def listed():
    names = tuple(PLACES)
    devices = np.arange(math.prod(PLACES.values())).reshape(tuple(PLACES.values()))
    return devices.transpose([names.index(name) for name in ORDER]).reshape(-1)


def time_table():
    t = np.arange(FLEN)
    f = np.arange(NF)
    hann = 0.5 - 0.5 * np.cos(2.0 * math.pi * t / FLEN)
    phases = 2.0 * math.pi / FLEN * ((f[:, None] * t[None, :]) % FLEN)
    factor = (0.375 * FLEN) ** -0.5
    table = np.stack([np.cos(phases), -np.sin(phases)], axis=0) * (hann * factor)
    table = table.reshape(2, BLOCKS, BINS, FLEN).transpose(1, 0, 2, 3)
    return table.reshape(2 * NF, FLEN).astype(ml_dtypes.bfloat16)


def dft_parts(length, sign):
    n = np.arange(length)
    phases = 2.0 * math.pi / length * ((n[:, None] * n[None, :]) % length)
    factor = length**-0.5
    return np.cos(phases) * factor, sign * np.sin(phases) * factor


def left_table(length, sign):
    re, im = dft_parts(length, sign)
    return np.block([[re, -im], [im, re]]).astype(ml_dtypes.bfloat16)


def right_table(length, sign):
    re, im = dft_parts(length, sign)
    return np.block([[re, im], [-im, re]]).astype(ml_dtypes.bfloat16)


def twiddle(sign):
    q = np.arange(N2)
    a = np.arange(N1)
    phases = 2.0 * math.pi / NCH * ((q[:, None] * a[None, :]) % NCH)
    return np.stack([np.cos(phases), sign * np.sin(phases)]).astype(np.float32)


def cosine_table():
    j = np.arange(NB)
    phases = math.pi / (2 * NB) * ((j[:, None] * (2 * j[None, :] + 1)) % (4 * NB))
    weight = np.where(j == 0, (1.0 / NB) ** 0.5, (2.0 / NB) ** 0.5)
    return (np.cos(phases) * weight[:, None]).astype(np.float32)


def band_weights(band_edges, freq):
    bounds = band_edges.astype(jnp.float32)
    freq = freq.astype(jnp.float32)[None, :]
    low, middle, high = bounds[:-2, None], bounds[1:-1, None], bounds[2:, None]
    rising = (freq - low) / (middle - low)
    falling = (high - freq) / (high - middle)
    return jnp.maximum(jnp.minimum(rising, falling), 0.0).astype(jnp.bfloat16)


def interval(band_edges, freq):
    below = jnp.sum((band_edges[None, :] <= freq[:, None]).astype(jnp.int32), axis=1)
    return jnp.minimum(below - 1, NB)


def spectrum_kernel(
    chunks,
    parts,
    table_hbm,
    traces_hbm,
    out_hbm,
    table,
    traces,
    out,
    table_sem,
    traces_sem,
    out_sem,
):
    rows = 2 * BINS
    height = 2 * NF // parts
    across = PLACES["x"] // parts
    lanes = SHARE * N1
    cores = PLACES["core"]
    width = SHARE * FLEN

    def table_copy(j):
        at = pl.ds(j * height, height)
        return pltpu.make_async_copy(table_hbm.at[at], table.at[at], table_sem.at[j])

    def traces_copy(i, core):
        at = pl.ds((i * cores + core) * width, width)
        return pltpu.make_async_copy(
            traces_hbm.at[:, at], traces.at[i, core], traces_sem.at[i, core]
        )

    def out_copy(i, j):
        at = (slice(None), slice(None), slice(None), pl.ds(j * across, across), i)
        return pltpu.make_async_copy(out.at[at], out_hbm.at[at], out_sem.at[i, j])

    traces_copy(0, 0).start()
    table_copy(0).start()
    traces_copy(0, 1).start()
    for j in range(1, parts):
        table_copy(j).start()
    for i in range(1, chunks):
        for core in range(cores):
            traces_copy(i, core).start()
    for i in range(chunks):
        for core in range(cores):
            traces_copy(i, core).wait()
        samples = jnp.concatenate(
            [
                traces[i, core, :, m * FLEN : (m + 1) * FLEN]
                for core in range(cores)
                for m in range(SHARE)
            ],
            axis=0,
        )
        for j in range(parts):
            if i == 0:
                table_copy(j).wait()
            part = lax.dot_general(
                table[j * height : (j + 1) * height, :],
                samples,
                (((1,), (1,)), ((), ())),
                preferred_element_type=jnp.float32,
            ).astype(jnp.bfloat16)
            for k in range(height // rows):
                block = j * (height // rows) + k
                x, zl, y = block // 8, block // 4 % 2, block % 4
                for core in range(cores):
                    out[zl, y, core, x, i] = part[
                        k * rows : (k + 1) * rows, core * lanes : (core + 1) * lanes
                    ]
            out_copy(i, j).start()
    for i in range(chunks):
        for j in range(parts):
            out_copy(i, j).wait()


def sections_kernel(
    cells_ref,
    first_ref,
    second_ref,
    third_ref,
    fourth_ref,
    forward_ref,
    inverse_ref,
    mask_ref,
    bands_ref,
    rounds_ref,
    sums_ref,
    rest_hbm,
    cells,
    turned,
    kept,
    back,
    power_rows,
    sums_f32,
    rest,
    rest_sem,
):
    group = 16
    step = 2
    bf16 = jnp.bfloat16
    dot = functools.partial(jnp.dot, preferred_element_type=jnp.float32)
    fwd_cos, fwd_sin = forward_ref[0], forward_ref[1]
    inv_cos, inv_sin = inverse_ref[0], inverse_ref[1]

    def band_sums(r):
        for m in range(2):
            for g in range(0, N2 // group, 2):
                power = jnp.concatenate(
                    [
                        power_rows[m, :, (g + i) * group : (g + i + 1) * group, :].reshape(
                            BINS * group, N1
                        )
                        for i in range(2)
                    ],
                    axis=1,
                )
                sums = dot(bands_ref[r], power)
                for i in range(2):
                    sums_f32[
                        (g + i) * group : (g + i + 1) * group, m * ROUND : (m + 1) * ROUND, :
                    ] = sums[:, i * N1 : (i + 1) * N1].reshape(group, ROUND, N1)

    for m in range(2):
        for g in range(N2 // group):
            for x in range(2):
                block = cells_ref[
                    g * group : (g + 1) * group,
                    x * BINS : (x + 1) * BINS,
                    m * N1 : (m + 1) * N1,
                ]
                block = jnp.swapaxes(block, 0, 1)
                for f in range(BINS):
                    cells[
                        x * N2 + g * group : x * N2 + (g + 1) * group, f * N1 : (f + 1) * N1
                    ] = block[f]
        for f0 in range(0, BINS, step):
            summed = dot(first_ref[...], cells[:, f0 * N1 : (f0 + step) * N1])
            for i in range(step):
                f = f0 + i
                re = summed[:N2, i * N1 : (i + 1) * N1]
                im = summed[N2:, i * N1 : (i + 1) * N1]
                turned[f * N2 : (f + 1) * N2, :N1] = (re * fwd_cos - im * fwd_sin).astype(bf16)
                turned[f * N2 : (f + 1) * N2, N1:] = (re * fwd_sin + im * fwd_cos).astype(bf16)
        for f0 in range(0, BINS, step):
            section = dot(turned[f0 * N2 : (f0 + step) * N2, :], second_ref[...]).astype(bf16)
            for i in range(step):
                f = f0 + i
                mask = mask_ref[f]
                for x in range(2):
                    kept[f * N2 : (f + 1) * N2, x * N1 : (x + 1) * N1] = (
                        section[i * N2 : (i + 1) * N2, x * N1 : (x + 1) * N1] * mask
                    )
        for f0 in range(0, BINS, step):
            summed = dot(kept[f0 * N2 : (f0 + step) * N2, :], third_ref[...])
            for i in range(step):
                f = f0 + i
                re = summed[i * N2 : (i + 1) * N2, :N1]
                im = summed[i * N2 : (i + 1) * N2, N1:]
                back[:N2, f * N1 : (f + 1) * N1] = (re * inv_cos - im * inv_sin).astype(bf16)
                back[N2:, f * N1 : (f + 1) * N1] = (re * inv_sin + im * inv_cos).astype(bf16)
        for f0 in range(0, BINS, step):
            filtered = dot(fourth_ref[...], back[:, f0 * N1 : (f0 + step) * N1])
            filtered = filtered.astype(bf16).astype(jnp.float32)
            power = filtered[:N2] * filtered[:N2] + filtered[N2:] * filtered[N2:]
            for i in range(step):
                power_rows[m, f0 + i] = power[:, i * N1 : (i + 1) * N1].astype(bf16)
    band_sums(0)
    sums_ref[...] = sums_f32[...].astype(bf16)
    at = pl.ds(pl.multiple_of(pl.program_id(0) * 2 * ROUND, 2 * ROUND), 2 * ROUND)
    for r in range(1, ROUNDS):

        @pl.when(rounds_ref[0] > r)
        def _():
            band_sums(r)
            rest[...] = sums_f32[...].astype(bf16)
            copy = pltpu.make_async_copy(rest, rest_hbm.at[r - 1, :, at, :], rest_sem)
            copy.start()
            copy.wait()


def shares_beside(received):
    sizes = tuple(PLACES[name] for name in ORDER)
    received = received.reshape(*sizes, SHARE * ROUND, N1)
    parts = [
        received[:, :, core, :, zh].reshape(BLOCKS * SHARE * ROUND, N1)
        for zh in range(PLACES["zh"])
        for core in range(PLACES["core"])
    ]
    return jnp.concatenate(parts, axis=1)


def band_places(firsts, r):
    band = firsts[:, None] + r * ROUND + jnp.arange(ROUND, dtype=jnp.int32)
    same = band[None, None, :, None, :] == jnp.arange(NB)[None, :, None, None, None]
    frames = jnp.eye(SHARE, dtype=bool)[:, None, None, :, None]
    return (same & frames).astype(jnp.bfloat16).reshape(SHARE * NB, BLOCKS * SHARE * ROUND)


def cepstra_kernel(sums_ref, places_ref, rest_ref, cosine_ref, out_ref):
    energy = jnp.dot(
        places_ref[...], shares_beside(sums_ref[...]), preferred_element_type=jnp.float32
    )
    logs = jnp.log(jnp.maximum(energy + rest_ref[...], energy_floor))
    for m in range(SHARE):
        cepstra = jnp.dot(
            cosine_ref[...],
            logs[m * NB : (m + 1) * NB],
            precision=lax.Precision.HIGHEST,
            preferred_element_type=jnp.float32,
        )
        for share in range(SHARES):
            out_ref[share * SHARE + m] = cepstra[:, share * N1 : (share + 1) * N1]


def whole(shape):
    return pl.BlockSpec(shape, lambda i: (0,) * len(shape))


VMEM_LIMIT = 48 * 1024 * 1024
VMEM_WHOLE = 60 * 1024 * 1024


def shards(traces, fan_mask, band_edges):
    devices = math.prod(lax.axis_size(name) for name in PLACES)
    sizes = tuple(PLACES[name] for name in ORDER)
    rows = 2 * BINS
    lanes = SHARE * N1
    order = np.concatenate([listed(), N2 + listed()])
    bf16 = jnp.bfloat16
    params = pltpu.CompilerParams(vmem_limit_bytes=VMEM_LIMIT)

    chunks, parts = PLACES["zh"], 2
    spectrum = pl.pallas_call(
        functools.partial(spectrum_kernel, chunks, parts),
        in_specs=[pl.BlockSpec(memory_space=pltpu.HBM)] * 2,
        out_specs=pl.BlockSpec(memory_space=pltpu.HBM),
        out_shape=jax.ShapeDtypeStruct((*sizes, rows, lanes), bf16),
        scratch_shapes=[
            pltpu.VMEM((2 * NF, FLEN), bf16),
            pltpu.VMEM((chunks, PLACES["core"], N1, SHARE * FLEN), bf16),
            pltpu.VMEM((*sizes, rows, lanes), bf16),
            pltpu.SemaphoreType.DMA((parts,)),
            pltpu.SemaphoreType.DMA((chunks, PLACES["core"])),
            pltpu.SemaphoreType.DMA((chunks, parts)),
        ],
        compiler_params=pltpu.CompilerParams(vmem_limit_bytes=VMEM_WHOLE),
        name="spectrum",
    )(jnp.asarray(time_table()), traces)
    spectrum = spectrum.reshape(devices, rows, lanes)

    cells = lax.all_to_all(spectrum, ORDER, split_axis=0, concat_axis=0, tiled=True)

    mask = jnp.transpose(fan_mask.reshape(BINS, N1, N2), (0, 2, 1))
    mask = (mask > 0).astype(bf16)

    blocks = np.arange(BLOCKS, dtype=np.int32).reshape(
        PLACES["x"], PLACES["zl"], PLACES["y"]
    )
    starts = jnp.asarray(blocks.transpose(1, 2, 0).reshape(-1) * BINS)
    firsts = interval(band_edges, starts) - 1
    touched = interval(band_edges, starts + BINS - 1) + 1 - firsts
    rounds = (jnp.max(touched) + ROUND - 1) // ROUND
    own = lax.axis_index(("x", "zl", "y"))
    weights = band_weights(band_edges, own * BINS + jnp.arange(BINS, dtype=jnp.int32))
    own_first = interval(band_edges, jnp.reshape(own * BINS, (1,))) - 1
    sent = own_first + jnp.arange(ROUNDS * ROUND, dtype=jnp.int32)
    chosen = sent[:, None] == jnp.arange(NB, dtype=jnp.int32)[None, :]
    weights = jnp.max(
        jnp.where(chosen[:, :, None], weights[None], jnp.zeros((), bf16)), axis=1
    )
    weights = weights.reshape(ROUNDS, 1, ROUND, BINS, 1)
    same = jnp.eye(16, dtype=bool)[None, :, None, None, :]
    bands = jnp.where(same, weights, jnp.zeros((), bf16)).reshape(
        ROUNDS, 16 * ROUND, BINS * 16
    )

    sums, rest = pl.pallas_call(
        sections_kernel,
        grid=(SHARE // 2,),
        in_specs=[
            pl.BlockSpec((N2, rows, 2 * N1), lambda i: (0, 0, i)),
            whole((2 * N2, 2 * N2)),
            whole((2 * N1, 2 * N1)),
            whole((2 * N1, 2 * N1)),
            whole((2 * N2, 2 * N2)),
            whole((2, N2, N1)),
            whole((2, N2, N1)),
            whole((BINS, N2, N1)),
            whole((ROUNDS, 16 * ROUND, BINS * 16)),
            pl.BlockSpec(memory_space=pltpu.SMEM),
        ],
        out_specs=[
            pl.BlockSpec((N2, 2 * ROUND, N1), lambda i: (0, i, 0)),
            pl.BlockSpec(memory_space=pltpu.HBM),
        ],
        out_shape=[
            jax.ShapeDtypeStruct((N2, SHARE * ROUND, N1), bf16),
            jax.ShapeDtypeStruct((ROUNDS - 1, N2, SHARE * ROUND, N1), bf16),
        ],
        scratch_shapes=[
            pltpu.VMEM((2 * N2, BINS * N1), bf16),
            pltpu.VMEM((BINS * N2, 2 * N1), bf16),
            pltpu.VMEM((BINS * N2, 2 * N1), bf16),
            pltpu.VMEM((2 * N2, BINS * N1), bf16),
            pltpu.VMEM((2, BINS, N2, N1), bf16),
            pltpu.VMEM((N2, 2 * ROUND, N1), jnp.float32),
            pltpu.VMEM((N2, 2 * ROUND, N1), bf16),
            pltpu.SemaphoreType.DMA,
        ],
        compiler_params=params,
        name="sections",
    )(
        cells,
        jnp.asarray(left_table(N2, -1.0)[:, order]),
        jnp.asarray(right_table(N1, -1.0)),
        jnp.asarray(right_table(N1, 1.0)),
        jnp.asarray(left_table(N2, 1.0)[order]),
        jnp.asarray(twiddle(-1.0)),
        jnp.asarray(twiddle(1.0)),
        mask,
        bands,
        jnp.reshape(rounds, (1,)),
    )

    def send(sums):
        return lax.all_to_all(sums, ORDER, split_axis=0, concat_axis=0, tiled=True)

    def further_round(r, energy):
        received = send(lax.dynamic_index_in_dim(rest, r - 1, 0, keepdims=False))
        return energy + jnp.dot(
            band_places(firsts, r), shares_beside(received), preferred_element_type=jnp.float32
        )

    further = lax.fori_loop(
        1, rounds, further_round, jnp.zeros((SHARE * NB, SHARES * N1), jnp.float32)
    )
    return pl.pallas_call(
        cepstra_kernel,
        in_specs=[pl.BlockSpec(memory_space=pltpu.VMEM)] * 4,
        out_specs=pl.BlockSpec(memory_space=pltpu.VMEM),
        out_shape=jax.ShapeDtypeStruct((FRAMES, NB, N1), jnp.float32),
        compiler_params=params,
        name="cepstra",
    )(send(sums), band_places(firsts, 0), further, jnp.asarray(cosine_table()))


def solution(mesh):
    places = Mesh(mesh.devices.reshape(tuple(PLACES.values())), tuple(PLACES))
    whole_axes = tuple(PLACES)
    in_specs = (P(whole_axes, None), P(("x", "zl", "y"), None), P())
    out_specs = P(None, None, whole_axes)
    return jax.shard_map(
        shards, mesh=places, in_specs=in_specs, out_specs=out_specs, check_vma=False
    )
```

```python
import functools
import math

import jax
import jax.numpy as jnp
import ml_dtypes
import numpy as np
from jax import lax
from jax.experimental import pallas as pl
from jax.experimental.pallas import tpu as pltpu
from jax.sharding import Mesh
from jax.sharding import PartitionSpec as P

NCH = 16384
N1 = 128
N2 = 128
FLEN = 1024
NF = 512
NB = 64
FRAMES = 16
BLOCKS = 32
BINS = NF // BLOCKS
SHARES = 4
SHARE = FRAMES // SHARES
ROUND = 8
ROUNDS = -(-(BINS + 1) // ROUND)

energy_floor = 0.05

PLACES = {"x": 4, "zl": 2, "y": 4, "zh": 2, "core": 2}
ORDER = ("zl", "y", "core", "x", "zh")


def listed():
    names = tuple(PLACES)
    devices = np.arange(math.prod(PLACES.values())).reshape(tuple(PLACES.values()))
    return devices.transpose([names.index(name) for name in ORDER]).reshape(-1)


def time_table():
    t = np.arange(FLEN)
    f = np.arange(NF)
    hann = 0.5 - 0.5 * np.cos(2.0 * math.pi * t / FLEN)
    phases = 2.0 * math.pi / FLEN * ((f[:, None] * t[None, :]) % FLEN)
    factor = (0.375 * FLEN) ** -0.5
    table = np.stack([np.cos(phases), -np.sin(phases)], axis=0) * (hann * factor)
    table = table.reshape(2, BLOCKS, BINS, FLEN).transpose(1, 0, 2, 3)
    return table.reshape(2 * NF, FLEN).astype(ml_dtypes.bfloat16)


def dft_parts(length, sign):
    n = np.arange(length)
    phases = 2.0 * math.pi / length * ((n[:, None] * n[None, :]) % length)
    factor = length**-0.5
    return np.cos(phases) * factor, sign * np.sin(phases) * factor


def left_table(length, sign):
    re, im = dft_parts(length, sign)
    return np.block([[re, -im], [im, re]]).astype(ml_dtypes.bfloat16)


def right_table(length, sign):
    re, im = dft_parts(length, sign)
    return np.block([[re, im], [-im, re]]).astype(ml_dtypes.bfloat16)


def twiddle(sign):
    q = np.arange(N2)
    a = np.arange(N1)
    phases = 2.0 * math.pi / NCH * ((q[:, None] * a[None, :]) % NCH)
    return np.stack([np.cos(phases), sign * np.sin(phases)]).astype(np.float32)


def cosine_table():
    j = np.arange(NB)
    phases = math.pi / (2 * NB) * ((j[:, None] * (2 * j[None, :] + 1)) % (4 * NB))
    weight = np.where(j == 0, (1.0 / NB) ** 0.5, (2.0 / NB) ** 0.5)
    return (np.cos(phases) * weight[:, None]).astype(np.float32)


def band_weights(band_edges, freq):
    bounds = band_edges.astype(jnp.float32)
    freq = freq.astype(jnp.float32)[None, :]
    low, middle, high = bounds[:-2, None], bounds[1:-1, None], bounds[2:, None]
    rising = (freq - low) / (middle - low)
    falling = (high - freq) / (high - middle)
    return jnp.maximum(jnp.minimum(rising, falling), 0.0).astype(jnp.bfloat16)


def interval(band_edges, freq):
    below = jnp.sum((band_edges[None, :] <= freq[:, None]).astype(jnp.int32), axis=1)
    return jnp.minimum(below - 1, NB)


def spectrum_kernel(
    chunks,
    parts,
    table_hbm,
    traces_hbm,
    out_hbm,
    table,
    traces,
    out,
    table_sem,
    traces_sem,
    out_sem,
):
    rows = 2 * BINS
    height = 2 * NF // parts
    across = PLACES["x"] // parts
    lanes = SHARE * N1
    cores = PLACES["core"]
    width = SHARE * FLEN

    def table_copy(j):
        at = pl.ds(j * height, height)
        return pltpu.make_async_copy(table_hbm.at[at], table.at[at], table_sem.at[j])

    def traces_copy(i, core):
        at = pl.ds((i * cores + core) * width, width)
        return pltpu.make_async_copy(
            traces_hbm.at[:, at], traces.at[i, core], traces_sem.at[i, core]
        )

    def out_copy(i, j):
        at = (slice(None), slice(None), slice(None), pl.ds(j * across, across), i)
        return pltpu.make_async_copy(out.at[at], out_hbm.at[at], out_sem.at[i, j])

    traces_copy(0, 0).start()
    table_copy(0).start()
    traces_copy(0, 1).start()
    for j in range(1, parts):
        table_copy(j).start()
    for i in range(1, chunks):
        for core in range(cores):
            traces_copy(i, core).start()
    for i in range(chunks):
        for core in range(cores):
            traces_copy(i, core).wait()
        samples = jnp.concatenate(
            [
                traces[i, core, :, m * FLEN : (m + 1) * FLEN]
                for core in range(cores)
                for m in range(SHARE)
            ],
            axis=0,
        )
        for j in range(parts):
            if i == 0:
                table_copy(j).wait()
            part = lax.dot_general(
                table[j * height : (j + 1) * height, :],
                samples,
                (((1,), (1,)), ((), ())),
                preferred_element_type=jnp.float32,
            ).astype(jnp.bfloat16)
            for k in range(height // rows):
                block = j * (height // rows) + k
                x, zl, y = block // 8, block // 4 % 2, block % 4
                for core in range(cores):
                    out[zl, y, core, x, i] = part[
                        k * rows : (k + 1) * rows, core * lanes : (core + 1) * lanes
                    ]
            out_copy(i, j).start()
    for i in range(chunks):
        for j in range(parts):
            out_copy(i, j).wait()


def sections_kernel(
    cells_ref,
    first_ref,
    second_ref,
    third_ref,
    fourth_ref,
    forward_ref,
    inverse_ref,
    mask_ref,
    bands_ref,
    rounds_ref,
    sums_ref,
    rest_hbm,
    cells,
    turned,
    kept,
    back,
    power_rows,
    sums_f32,
    rest,
    rest_sem,
):
    group = 16
    step = 2
    bf16 = jnp.bfloat16
    dot = functools.partial(jnp.dot, preferred_element_type=jnp.float32)
    fwd_cos, fwd_sin = forward_ref[0], forward_ref[1]
    inv_cos, inv_sin = inverse_ref[0], inverse_ref[1]

    def band_sums(r):
        for m in range(2):
            for g in range(0, N2 // group, 2):
                power = jnp.concatenate(
                    [
                        power_rows[m, :, (g + i) * group : (g + i + 1) * group, :].reshape(
                            BINS * group, N1
                        )
                        for i in range(2)
                    ],
                    axis=1,
                )
                sums = dot(bands_ref[r], power)
                for i in range(2):
                    sums_f32[
                        (g + i) * group : (g + i + 1) * group, m * ROUND : (m + 1) * ROUND, :
                    ] = sums[:, i * N1 : (i + 1) * N1].reshape(group, ROUND, N1)

    for m in range(2):
        for g in range(N2 // group):
            for x in range(2):
                block = cells_ref[
                    g * group : (g + 1) * group,
                    x * BINS : (x + 1) * BINS,
                    m * N1 : (m + 1) * N1,
                ]
                block = jnp.swapaxes(block, 0, 1)
                for f in range(BINS):
                    cells[
                        x * N2 + g * group : x * N2 + (g + 1) * group, f * N1 : (f + 1) * N1
                    ] = block[f]
        for f0 in range(0, BINS, step):
            summed = dot(first_ref[...], cells[:, f0 * N1 : (f0 + step) * N1])
            for i in range(step):
                f = f0 + i
                re = summed[:N2, i * N1 : (i + 1) * N1]
                im = summed[N2:, i * N1 : (i + 1) * N1]
                turned[f * N2 : (f + 1) * N2, :N1] = (re * fwd_cos - im * fwd_sin).astype(bf16)
                turned[f * N2 : (f + 1) * N2, N1:] = (re * fwd_sin + im * fwd_cos).astype(bf16)
        for f0 in range(0, BINS, step):
            section = dot(turned[f0 * N2 : (f0 + step) * N2, :], second_ref[...]).astype(bf16)
            for i in range(step):
                f = f0 + i
                mask = mask_ref[f]
                for x in range(2):
                    kept[f * N2 : (f + 1) * N2, x * N1 : (x + 1) * N1] = (
                        section[i * N2 : (i + 1) * N2, x * N1 : (x + 1) * N1] * mask
                    )
        for f0 in range(0, BINS, step):
            summed = dot(kept[f0 * N2 : (f0 + step) * N2, :], third_ref[...])
            for i in range(step):
                f = f0 + i
                re = summed[i * N2 : (i + 1) * N2, :N1]
                im = summed[i * N2 : (i + 1) * N2, N1:]
                back[:N2, f * N1 : (f + 1) * N1] = (re * inv_cos - im * inv_sin).astype(bf16)
                back[N2:, f * N1 : (f + 1) * N1] = (re * inv_sin + im * inv_cos).astype(bf16)
        for f0 in range(0, BINS, step):
            filtered = dot(fourth_ref[...], back[:, f0 * N1 : (f0 + step) * N1])
            filtered = filtered.astype(bf16).astype(jnp.float32)
            power = filtered[:N2] * filtered[:N2] + filtered[N2:] * filtered[N2:]
            for i in range(step):
                power_rows[m, f0 + i] = power[:, i * N1 : (i + 1) * N1].astype(bf16)
    band_sums(0)
    sums_ref[...] = sums_f32[...].astype(bf16)
    at = pl.ds(pl.multiple_of(pl.program_id(0) * 2 * ROUND, 2 * ROUND), 2 * ROUND)
    for r in range(1, ROUNDS):

        @pl.when(rounds_ref[0] > r)
        def _():
            band_sums(r)
            rest[...] = sums_f32[...].astype(bf16)
            copy = pltpu.make_async_copy(rest, rest_hbm.at[r - 1, :, at, :], rest_sem)
            copy.start()
            copy.wait()


def shares_beside(received):
    sizes = tuple(PLACES[name] for name in ORDER)
    received = received.reshape(*sizes, SHARE * ROUND, N1)
    parts = [
        received[:, :, core, :, zh].reshape(BLOCKS * SHARE * ROUND, N1)
        for zh in range(PLACES["zh"])
        for core in range(PLACES["core"])
    ]
    return jnp.concatenate(parts, axis=1)


def band_places(firsts, r):
    band = firsts[:, None] + r * ROUND + jnp.arange(ROUND, dtype=jnp.int32)
    same = band[None, None, :, None, :] == jnp.arange(NB)[None, :, None, None, None]
    frames = jnp.eye(SHARE, dtype=bool)[:, None, None, :, None]
    return (same & frames).astype(jnp.bfloat16).reshape(SHARE * NB, BLOCKS * SHARE * ROUND)


def cepstra_kernel(sums_ref, places_ref, rest_ref, cosine_ref, out_ref):
    energy = jnp.dot(
        places_ref[...], shares_beside(sums_ref[...]), preferred_element_type=jnp.float32
    )
    logs = jnp.log(jnp.maximum(energy + rest_ref[...], energy_floor))
    width = SHARES * N1
    logs = jnp.concatenate([logs[m * NB : (m + 1) * NB] for m in range(SHARE)], axis=1)
    bf16 = jnp.bfloat16
    dot = functools.partial(jnp.dot, preferred_element_type=jnp.float32)
    high = logs.astype(bf16)
    low = (logs - high.astype(jnp.float32)).astype(bf16)
    cosine = cosine_ref[...]
    cosine_high = cosine.astype(bf16)
    cosine_low = (cosine - cosine_high.astype(jnp.float32)).astype(bf16)
    left = jnp.concatenate([cosine_high, cosine_low, cosine_high], axis=1)
    right = jnp.concatenate([high, high, low], axis=0)
    cepstra = dot(left, right)
    for m in range(SHARE):
        for share in range(SHARES):
            at = m * width + share * N1
            out_ref[share * SHARE + m] = cepstra[:, at : at + N1]


def whole(shape):
    return pl.BlockSpec(shape, lambda i: (0,) * len(shape))


VMEM_LIMIT = 48 * 1024 * 1024
VMEM_WHOLE = 60 * 1024 * 1024


def shards(traces, fan_mask, band_edges):
    devices = math.prod(lax.axis_size(name) for name in PLACES)
    sizes = tuple(PLACES[name] for name in ORDER)
    rows = 2 * BINS
    lanes = SHARE * N1
    order = np.concatenate([listed(), N2 + listed()])
    bf16 = jnp.bfloat16
    params = pltpu.CompilerParams(vmem_limit_bytes=VMEM_LIMIT)

    chunks, parts = PLACES["zh"], 2
    spectrum = pl.pallas_call(
        functools.partial(spectrum_kernel, chunks, parts),
        in_specs=[pl.BlockSpec(memory_space=pltpu.HBM)] * 2,
        out_specs=pl.BlockSpec(memory_space=pltpu.HBM),
        out_shape=jax.ShapeDtypeStruct((*sizes, rows, lanes), bf16),
        scratch_shapes=[
            pltpu.VMEM((2 * NF, FLEN), bf16),
            pltpu.VMEM((chunks, PLACES["core"], N1, SHARE * FLEN), bf16),
            pltpu.VMEM((*sizes, rows, lanes), bf16),
            pltpu.SemaphoreType.DMA((parts,)),
            pltpu.SemaphoreType.DMA((chunks, PLACES["core"])),
            pltpu.SemaphoreType.DMA((chunks, parts)),
        ],
        compiler_params=pltpu.CompilerParams(vmem_limit_bytes=VMEM_WHOLE),
        name="spectrum",
    )(jnp.asarray(time_table()), traces)
    spectrum = spectrum.reshape(devices, rows, lanes)

    cells = lax.all_to_all(spectrum, ORDER, split_axis=0, concat_axis=0, tiled=True)

    mask = jnp.transpose(fan_mask.reshape(BINS, N1, N2), (0, 2, 1))
    mask = (mask > 0).astype(bf16)

    blocks = np.arange(BLOCKS, dtype=np.int32).reshape(
        PLACES["x"], PLACES["zl"], PLACES["y"]
    )
    starts = jnp.asarray(blocks.transpose(1, 2, 0).reshape(-1) * BINS)
    firsts = interval(band_edges, starts) - 1
    touched = interval(band_edges, starts + BINS - 1) + 1 - firsts
    rounds = (jnp.max(touched) + ROUND - 1) // ROUND
    own = lax.axis_index(("x", "zl", "y"))
    weights = band_weights(band_edges, own * BINS + jnp.arange(BINS, dtype=jnp.int32))
    own_first = interval(band_edges, jnp.reshape(own * BINS, (1,))) - 1
    sent = own_first + jnp.arange(ROUNDS * ROUND, dtype=jnp.int32)
    chosen = sent[:, None] == jnp.arange(NB, dtype=jnp.int32)[None, :]
    weights = jnp.max(
        jnp.where(chosen[:, :, None], weights[None], jnp.zeros((), bf16)), axis=1
    )
    weights = weights.reshape(ROUNDS, 1, ROUND, BINS, 1)
    same = jnp.eye(16, dtype=bool)[None, :, None, None, :]
    bands = jnp.where(same, weights, jnp.zeros((), bf16)).reshape(
        ROUNDS, 16 * ROUND, BINS * 16
    )

    sums, rest = pl.pallas_call(
        sections_kernel,
        grid=(SHARE // 2,),
        in_specs=[
            pl.BlockSpec((N2, rows, 2 * N1), lambda i: (0, 0, i)),
            whole((2 * N2, 2 * N2)),
            whole((2 * N1, 2 * N1)),
            whole((2 * N1, 2 * N1)),
            whole((2 * N2, 2 * N2)),
            whole((2, N2, N1)),
            whole((2, N2, N1)),
            whole((BINS, N2, N1)),
            whole((ROUNDS, 16 * ROUND, BINS * 16)),
            pl.BlockSpec(memory_space=pltpu.SMEM),
        ],
        out_specs=[
            pl.BlockSpec((N2, 2 * ROUND, N1), lambda i: (0, i, 0)),
            pl.BlockSpec(memory_space=pltpu.HBM),
        ],
        out_shape=[
            jax.ShapeDtypeStruct((N2, SHARE * ROUND, N1), bf16),
            jax.ShapeDtypeStruct((ROUNDS - 1, N2, SHARE * ROUND, N1), bf16),
        ],
        scratch_shapes=[
            pltpu.VMEM((2 * N2, BINS * N1), bf16),
            pltpu.VMEM((BINS * N2, 2 * N1), bf16),
            pltpu.VMEM((BINS * N2, 2 * N1), bf16),
            pltpu.VMEM((2 * N2, BINS * N1), bf16),
            pltpu.VMEM((2, BINS, N2, N1), bf16),
            pltpu.VMEM((N2, 2 * ROUND, N1), jnp.float32),
            pltpu.VMEM((N2, 2 * ROUND, N1), bf16),
            pltpu.SemaphoreType.DMA,
        ],
        compiler_params=params,
        name="sections",
    )(
        cells,
        jnp.asarray(left_table(N2, -1.0)[:, order]),
        jnp.asarray(right_table(N1, -1.0)),
        jnp.asarray(right_table(N1, 1.0)),
        jnp.asarray(left_table(N2, 1.0)[order]),
        jnp.asarray(twiddle(-1.0)),
        jnp.asarray(twiddle(1.0)),
        mask,
        bands,
        jnp.reshape(rounds, (1,)),
    )

    def send(sums):
        return lax.all_to_all(sums, ORDER, split_axis=0, concat_axis=0, tiled=True)

    def further_round(r, energy):
        received = send(lax.dynamic_index_in_dim(rest, r - 1, 0, keepdims=False))
        return energy + jnp.dot(
            band_places(firsts, r), shares_beside(received), preferred_element_type=jnp.float32
        )

    further = lax.fori_loop(
        1, rounds, further_round, jnp.zeros((SHARE * NB, SHARES * N1), jnp.float32)
    )
    return pl.pallas_call(
        cepstra_kernel,
        in_specs=[pl.BlockSpec(memory_space=pltpu.VMEM)] * 4,
        out_specs=pl.BlockSpec(memory_space=pltpu.VMEM),
        out_shape=jax.ShapeDtypeStruct((FRAMES, NB, N1), jnp.float32),
        compiler_params=params,
        name="cepstra",
    )(send(sums), band_places(firsts, 0), further, jnp.asarray(cosine_table()))


def solution(mesh):
    places = Mesh(mesh.devices.reshape(tuple(PLACES.values())), tuple(PLACES))
    whole_axes = tuple(PLACES)
    in_specs = (P(whole_axes, None), P(("x", "zl", "y"), None), P())
    out_specs = P(None, None, whole_axes)
    return jax.shard_map(
        shards, mesh=places, in_specs=in_specs, out_specs=out_specs, check_vma=False
    )
```

```python
import functools
import math

import jax
import jax.numpy as jnp
import ml_dtypes
import numpy as np
from jax import lax
from jax.experimental import pallas as pl
from jax.experimental.pallas import tpu as pltpu
from jax.sharding import Mesh
from jax.sharding import PartitionSpec as P

NCH = 16384
N1 = 128
N2 = 128
FLEN = 1024
NF = 512
NB = 64
FRAMES = 16
BLOCKS = 32
BINS = NF // BLOCKS
SHARES = 4
SHARE = FRAMES // SHARES
ROUND = 8
ROUNDS = -(-(BINS + 1) // ROUND)

energy_floor = 0.05

PLACES = {"x": 4, "zl": 2, "y": 4, "zh": 2, "core": 2}
ORDER = ("zl", "y", "core", "x", "zh")


def listed():
    names = tuple(PLACES)
    devices = np.arange(math.prod(PLACES.values())).reshape(tuple(PLACES.values()))
    return devices.transpose([names.index(name) for name in ORDER]).reshape(-1)


def time_table():
    t = np.arange(FLEN)
    f = np.arange(NF)
    hann = 0.5 - 0.5 * np.cos(2.0 * math.pi * t / FLEN)
    phases = 2.0 * math.pi / FLEN * ((f[:, None] * t[None, :]) % FLEN)
    factor = (0.375 * FLEN) ** -0.5
    table = np.stack([np.cos(phases), -np.sin(phases)], axis=0) * (hann * factor)
    table = table.reshape(2, BLOCKS, BINS, FLEN).transpose(1, 0, 2, 3)
    return table.reshape(2 * NF, FLEN).astype(ml_dtypes.bfloat16)


def dft_parts(length, sign):
    n = np.arange(length)
    phases = 2.0 * math.pi / length * ((n[:, None] * n[None, :]) % length)
    factor = length**-0.5
    return np.cos(phases) * factor, sign * np.sin(phases) * factor


def left_table(length, sign):
    re, im = dft_parts(length, sign)
    return np.block([[re, -im], [im, re]]).astype(ml_dtypes.bfloat16)


def right_table(length, sign):
    re, im = dft_parts(length, sign)
    return np.block([[re, im], [-im, re]]).astype(ml_dtypes.bfloat16)


def twiddle(sign):
    q = np.arange(N2)
    a = np.arange(N1)
    phases = 2.0 * math.pi / NCH * ((q[:, None] * a[None, :]) % NCH)
    return np.stack([np.cos(phases), sign * np.sin(phases)]).astype(np.float32)


def cosine_table():
    j = np.arange(NB)
    phases = math.pi / (2 * NB) * ((j[:, None] * (2 * j[None, :] + 1)) % (4 * NB))
    weight = np.where(j == 0, (1.0 / NB) ** 0.5, (2.0 / NB) ** 0.5)
    return (np.cos(phases) * weight[:, None]).astype(np.float32)


def band_weights(band_edges, freq):
    bounds = band_edges.astype(jnp.float32)
    freq = freq.astype(jnp.float32)[None, :]
    low, middle, high = bounds[:-2, None], bounds[1:-1, None], bounds[2:, None]
    rising = (freq - low) / (middle - low)
    falling = (high - freq) / (high - middle)
    return jnp.maximum(jnp.minimum(rising, falling), 0.0).astype(jnp.bfloat16)


def interval(band_edges, freq):
    below = jnp.sum((band_edges[None, :] <= freq[:, None]).astype(jnp.int32), axis=1)
    return jnp.minimum(below - 1, NB)


def spectrum_kernel(
    chunks,
    parts,
    table_hbm,
    traces_hbm,
    out_hbm,
    table,
    traces,
    out,
    table_sem,
    traces_sem,
    out_sem,
):
    rows = 2 * BINS
    height = 2 * NF // parts
    across = PLACES["x"] // parts
    lanes = SHARE * N1
    cores = PLACES["core"]
    width = SHARE * FLEN

    def table_copy(j):
        at = pl.ds(j * height, height)
        return pltpu.make_async_copy(table_hbm.at[at], table.at[at], table_sem.at[j])

    def traces_copy(i, core):
        at = pl.ds((i * cores + core) * width, width)
        return pltpu.make_async_copy(
            traces_hbm.at[:, at], traces.at[i, core], traces_sem.at[i, core]
        )

    def out_copy(i, j):
        at = (slice(None), slice(None), slice(None), pl.ds(j * across, across), i)
        return pltpu.make_async_copy(out.at[at], out_hbm.at[at], out_sem.at[i, j])

    traces_copy(0, 0).start()
    table_copy(0).start()
    traces_copy(0, 1).start()
    for j in range(1, parts):
        table_copy(j).start()
    for i in range(1, chunks):
        for core in range(cores):
            traces_copy(i, core).start()
    for i in range(chunks):
        for core in range(cores):
            traces_copy(i, core).wait()
        samples = jnp.concatenate(
            [
                traces[i, core, :, m * FLEN : (m + 1) * FLEN]
                for core in range(cores)
                for m in range(SHARE)
            ],
            axis=0,
        )
        for j in range(parts):
            if i == 0:
                table_copy(j).wait()
            part = lax.dot_general(
                table[j * height : (j + 1) * height, :],
                samples,
                (((1,), (1,)), ((), ())),
                preferred_element_type=jnp.float32,
            ).astype(jnp.bfloat16)
            for k in range(height // rows):
                block = j * (height // rows) + k
                x, zl, y = block // 8, block // 4 % 2, block % 4
                for core in range(cores):
                    out[zl, y, core, x, i] = part[
                        k * rows : (k + 1) * rows, core * lanes : (core + 1) * lanes
                    ]
            out_copy(i, j).start()
    for i in range(chunks):
        for j in range(parts):
            out_copy(i, j).wait()


def sections_kernel(
    cells_ref,
    first_ref,
    second_ref,
    third_ref,
    fourth_ref,
    forward_ref,
    inverse_ref,
    mask_ref,
    bands_ref,
    rounds_ref,
    sums_ref,
    rest_hbm,
    cells,
    turned,
    kept,
    back,
    power_rows,
    sums_f32,
    rest,
    rest_sem,
):
    group = 16
    step = 2
    bf16 = jnp.bfloat16
    dot = functools.partial(jnp.dot, preferred_element_type=jnp.float32)
    fwd_cos, fwd_sin = forward_ref[0], forward_ref[1]
    inv_cos, inv_sin = inverse_ref[0], inverse_ref[1]

    def band_sums(r):
        for m in range(2):
            for g in range(0, N2 // group, 2):
                power = jnp.concatenate(
                    [
                        power_rows[m, :, (g + i) * group : (g + i + 1) * group, :].reshape(
                            BINS * group, N1
                        )
                        for i in range(2)
                    ],
                    axis=1,
                )
                sums = dot(bands_ref[r], power)
                for i in range(2):
                    sums_f32[
                        (g + i) * group : (g + i + 1) * group, m * ROUND : (m + 1) * ROUND, :
                    ] = sums[:, i * N1 : (i + 1) * N1].reshape(group, ROUND, N1)

    for m in range(2):
        for g in range(N2 // group):
            for x in range(2):
                block = cells_ref[
                    g * group : (g + 1) * group,
                    x * BINS : (x + 1) * BINS,
                    m * N1 : (m + 1) * N1,
                ]
                block = jnp.swapaxes(block, 0, 1)
                for f in range(BINS):
                    cells[
                        x * N2 + g * group : x * N2 + (g + 1) * group, f * N1 : (f + 1) * N1
                    ] = block[f]
        for f0 in range(0, BINS, step):
            summed = dot(first_ref[...], cells[:, f0 * N1 : (f0 + step) * N1])
            for i in range(step):
                f = f0 + i
                re = summed[:N2, i * N1 : (i + 1) * N1]
                im = summed[N2:, i * N1 : (i + 1) * N1]
                turned[f * N2 : (f + 1) * N2, :N1] = (re * fwd_cos - im * fwd_sin).astype(bf16)
                turned[f * N2 : (f + 1) * N2, N1:] = (re * fwd_sin + im * fwd_cos).astype(bf16)
        for f0 in range(0, BINS, step):
            section = dot(turned[f0 * N2 : (f0 + step) * N2, :], second_ref[...]).astype(bf16)
            for i in range(step):
                f = f0 + i
                mask = mask_ref[f]
                for x in range(2):
                    kept[f * N2 : (f + 1) * N2, x * N1 : (x + 1) * N1] = (
                        section[i * N2 : (i + 1) * N2, x * N1 : (x + 1) * N1] * mask
                    )
        for f0 in range(0, BINS, step):
            summed = dot(kept[f0 * N2 : (f0 + step) * N2, :], third_ref[...])
            for i in range(step):
                f = f0 + i
                re = summed[i * N2 : (i + 1) * N2, :N1]
                im = summed[i * N2 : (i + 1) * N2, N1:]
                back[:N2, f * N1 : (f + 1) * N1] = (re * inv_cos - im * inv_sin).astype(bf16)
                back[N2:, f * N1 : (f + 1) * N1] = (re * inv_sin + im * inv_cos).astype(bf16)
        for f0 in range(0, BINS, step):
            filtered = dot(fourth_ref[...], back[:, f0 * N1 : (f0 + step) * N1])
            filtered = filtered.astype(bf16).astype(jnp.float32)
            power = filtered[:N2] * filtered[:N2] + filtered[N2:] * filtered[N2:]
            for i in range(step):
                power_rows[m, f0 + i] = power[:, i * N1 : (i + 1) * N1].astype(bf16)
    band_sums(0)
    at = pl.ds(pl.multiple_of(pl.program_id(0) * 2 * ROUND, 2 * ROUND), 2 * ROUND)
    sums_ref[:, at, :] = sums_f32[...].astype(bf16)
    for r in range(1, ROUNDS):

        @pl.when(rounds_ref[0] > r)
        def _():
            band_sums(r)
            rest[...] = sums_f32[...].astype(bf16)
            copy = pltpu.make_async_copy(rest, rest_hbm.at[r - 1, :, at, :], rest_sem)
            copy.start()
            copy.wait()


def shares_beside(received):
    sizes = tuple(PLACES[name] for name in ORDER)
    received = received.reshape(*sizes, SHARE * ROUND, N1)
    parts = [
        received[:, :, core, :, zh].reshape(BLOCKS * SHARE * ROUND, N1)
        for zh in range(PLACES["zh"])
        for core in range(PLACES["core"])
    ]
    return jnp.concatenate(parts, axis=1)


def band_places(firsts, r):
    band = firsts[:, None] + r * ROUND + jnp.arange(ROUND, dtype=jnp.int32)
    same = band[None, None, :, None, :] == jnp.arange(NB)[None, :, None, None, None]
    frames = jnp.eye(SHARE, dtype=bool)[:, None, None, :, None]
    return (same & frames).astype(jnp.bfloat16).reshape(SHARE * NB, BLOCKS * SHARE * ROUND)


def cepstra_kernel(sums_ref, places_ref, rest_ref, cosine_ref, out_ref):
    energy = jnp.dot(
        places_ref[...], shares_beside(sums_ref[...]), preferred_element_type=jnp.float32
    )
    logs = jnp.log(jnp.maximum(energy + rest_ref[...], energy_floor))
    width = SHARES * N1
    logs = jnp.concatenate([logs[m * NB : (m + 1) * NB] for m in range(SHARE)], axis=1)
    bf16 = jnp.bfloat16
    dot = functools.partial(jnp.dot, preferred_element_type=jnp.float32)
    high = logs.astype(bf16)
    low = (logs - high.astype(jnp.float32)).astype(bf16)
    cosine = cosine_ref[...]
    cosine_high = cosine.astype(bf16)
    cosine_low = (cosine - cosine_high.astype(jnp.float32)).astype(bf16)
    left = jnp.concatenate([cosine_high, cosine_low, cosine_high], axis=1)
    right = jnp.concatenate([high, high, low], axis=0)
    cepstra = dot(left, right)
    for m in range(SHARE):
        for share in range(SHARES):
            at = m * width + share * N1
            out_ref[share * SHARE + m] = cepstra[:, at : at + N1]


def whole(shape):
    return pl.BlockSpec(shape, lambda i: (0,) * len(shape))


VMEM_LIMIT = 48 * 1024 * 1024
VMEM_WHOLE = 60 * 1024 * 1024


def shards(traces, fan_mask, band_edges):
    devices = math.prod(lax.axis_size(name) for name in PLACES)
    sizes = tuple(PLACES[name] for name in ORDER)
    rows = 2 * BINS
    lanes = SHARE * N1
    order = np.concatenate([listed(), N2 + listed()])
    bf16 = jnp.bfloat16
    params = pltpu.CompilerParams(vmem_limit_bytes=VMEM_LIMIT)

    chunks, parts = PLACES["zh"], 2
    spectrum = pl.pallas_call(
        functools.partial(spectrum_kernel, chunks, parts),
        in_specs=[pl.BlockSpec(memory_space=pltpu.HBM)] * 2,
        out_specs=pl.BlockSpec(memory_space=pltpu.HBM),
        out_shape=jax.ShapeDtypeStruct((*sizes, rows, lanes), bf16),
        scratch_shapes=[
            pltpu.VMEM((2 * NF, FLEN), bf16),
            pltpu.VMEM((chunks, PLACES["core"], N1, SHARE * FLEN), bf16),
            pltpu.VMEM((*sizes, rows, lanes), bf16),
            pltpu.SemaphoreType.DMA((parts,)),
            pltpu.SemaphoreType.DMA((chunks, PLACES["core"])),
            pltpu.SemaphoreType.DMA((chunks, parts)),
        ],
        compiler_params=pltpu.CompilerParams(vmem_limit_bytes=VMEM_WHOLE),
        name="spectrum",
    )(jnp.asarray(time_table()), traces)
    spectrum = spectrum.reshape(devices, rows, lanes)

    cells = lax.all_to_all(spectrum, ORDER, split_axis=0, concat_axis=0, tiled=True)

    mask = jnp.transpose(fan_mask.reshape(BINS, N1, N2), (0, 2, 1))
    mask = (mask > 0).astype(bf16)

    blocks = np.arange(BLOCKS, dtype=np.int32).reshape(
        PLACES["x"], PLACES["zl"], PLACES["y"]
    )
    starts = jnp.asarray(blocks.transpose(1, 2, 0).reshape(-1) * BINS)
    firsts = interval(band_edges, starts) - 1
    touched = interval(band_edges, starts + BINS - 1) + 1 - firsts
    rounds = (jnp.max(touched) + ROUND - 1) // ROUND
    own = lax.axis_index(("x", "zl", "y"))
    weights = band_weights(band_edges, own * BINS + jnp.arange(BINS, dtype=jnp.int32))
    own_first = interval(band_edges, jnp.reshape(own * BINS, (1,))) - 1
    sent = own_first + jnp.arange(ROUNDS * ROUND, dtype=jnp.int32)
    chosen = sent[:, None] == jnp.arange(NB, dtype=jnp.int32)[None, :]
    weights = jnp.max(
        jnp.where(chosen[:, :, None], weights[None], jnp.zeros((), bf16)), axis=1
    )
    weights = weights.reshape(ROUNDS, 1, ROUND, BINS, 1)
    same = jnp.eye(16, dtype=bool)[None, :, None, None, :]
    bands = jnp.where(same, weights, jnp.zeros((), bf16)).reshape(
        ROUNDS, 16 * ROUND, BINS * 16
    )

    sums, rest = pl.pallas_call(
        sections_kernel,
        grid=(SHARE // 2,),
        in_specs=[
            pl.BlockSpec((N2, rows, 2 * N1), lambda i: (0, 0, i)),
            whole((2 * N2, 2 * N2)),
            whole((2 * N1, 2 * N1)),
            whole((2 * N1, 2 * N1)),
            whole((2 * N2, 2 * N2)),
            whole((2, N2, N1)),
            whole((2, N2, N1)),
            whole((BINS, N2, N1)),
            whole((ROUNDS, 16 * ROUND, BINS * 16)),
            pl.BlockSpec(memory_space=pltpu.SMEM),
        ],
        out_specs=[
            pl.BlockSpec(memory_space=pltpu.VMEM),
            pl.BlockSpec(memory_space=pltpu.HBM),
        ],
        out_shape=[
            jax.ShapeDtypeStruct((N2, SHARE * ROUND, N1), bf16),
            jax.ShapeDtypeStruct((ROUNDS - 1, N2, SHARE * ROUND, N1), bf16),
        ],
        scratch_shapes=[
            pltpu.VMEM((2 * N2, BINS * N1), bf16),
            pltpu.VMEM((BINS * N2, 2 * N1), bf16),
            pltpu.VMEM((BINS * N2, 2 * N1), bf16),
            pltpu.VMEM((2 * N2, BINS * N1), bf16),
            pltpu.VMEM((2, BINS, N2, N1), bf16),
            pltpu.VMEM((N2, 2 * ROUND, N1), jnp.float32),
            pltpu.VMEM((N2, 2 * ROUND, N1), bf16),
            pltpu.SemaphoreType.DMA,
        ],
        compiler_params=params,
        name="sections",
    )(
        cells,
        jnp.asarray(left_table(N2, -1.0)[:, order]),
        jnp.asarray(right_table(N1, -1.0)),
        jnp.asarray(right_table(N1, 1.0)),
        jnp.asarray(left_table(N2, 1.0)[order]),
        jnp.asarray(twiddle(-1.0)),
        jnp.asarray(twiddle(1.0)),
        mask,
        bands,
        jnp.reshape(rounds, (1,)),
    )

    def send(sums):
        return lax.all_to_all(sums, ORDER, split_axis=0, concat_axis=0, tiled=True)

    def further_round(r, energy):
        received = send(lax.dynamic_index_in_dim(rest, r - 1, 0, keepdims=False))
        return energy + jnp.dot(
            band_places(firsts, r), shares_beside(received), preferred_element_type=jnp.float32
        )

    further = lax.fori_loop(
        1, rounds, further_round, jnp.zeros((SHARE * NB, SHARES * N1), jnp.float32)
    )
    return pl.pallas_call(
        cepstra_kernel,
        in_specs=[pl.BlockSpec(memory_space=pltpu.VMEM)] * 4,
        out_specs=pl.BlockSpec(memory_space=pltpu.VMEM),
        out_shape=jax.ShapeDtypeStruct((FRAMES, NB, N1), jnp.float32),
        compiler_params=params,
        name="cepstra",
    )(send(sums), band_places(firsts, 0), further, jnp.asarray(cosine_table()))


def solution(mesh):
    places = Mesh(mesh.devices.reshape(tuple(PLACES.values())), tuple(PLACES))
    whole_axes = tuple(PLACES)
    in_specs = (P(whole_axes, None), P(("x", "zl", "y"), None), P())
    out_specs = P(None, None, whole_axes)
    return jax.shard_map(
        shards, mesh=places, in_specs=in_specs, out_specs=out_specs, check_vma=False
    )
```

```python
import functools
import math

import jax
import jax.numpy as jnp
import ml_dtypes
import numpy as np
from jax import lax
from jax.experimental import pallas as pl
from jax.experimental.pallas import tpu as pltpu
from jax.sharding import Mesh
from jax.sharding import PartitionSpec as P

NCH = 16384
N1 = 128
N2 = 128
FLEN = 1024
NF = 512
NB = 64
FRAMES = 16
BLOCKS = 32
BINS = NF // BLOCKS
SHARES = 4
SHARE = FRAMES // SHARES
ROUND = 8
ROUNDS = -(-(BINS + 1) // ROUND)

energy_floor = 0.05

PLACES = {"x": 4, "zl": 2, "y": 4, "zh": 2, "core": 2}
ORDER = ("zl", "y", "core", "x", "zh")


def listed():
    names = tuple(PLACES)
    devices = np.arange(math.prod(PLACES.values())).reshape(tuple(PLACES.values()))
    return devices.transpose([names.index(name) for name in ORDER]).reshape(-1)


def time_table():
    t = np.arange(FLEN)
    f = np.arange(NF)
    hann = 0.5 - 0.5 * np.cos(2.0 * math.pi * t / FLEN)
    phases = 2.0 * math.pi / FLEN * ((f[:, None] * t[None, :]) % FLEN)
    factor = (0.375 * FLEN) ** -0.5
    table = np.stack([np.cos(phases), -np.sin(phases)], axis=0) * (hann * factor)
    table = table.reshape(2, BLOCKS, BINS, FLEN).transpose(1, 0, 2, 3)
    return table.reshape(2 * NF, FLEN).astype(ml_dtypes.bfloat16)


def dft_parts(length, sign):
    n = np.arange(length)
    phases = 2.0 * math.pi / length * ((n[:, None] * n[None, :]) % length)
    factor = length**-0.5
    return np.cos(phases) * factor, sign * np.sin(phases) * factor


def left_table(length, sign):
    re, im = dft_parts(length, sign)
    return np.block([[re, -im], [im, re]]).astype(ml_dtypes.bfloat16)


def right_table(length, sign):
    re, im = dft_parts(length, sign)
    return np.block([[re, im], [-im, re]]).astype(ml_dtypes.bfloat16)


def twiddle(sign):
    q = np.arange(N2)
    a = np.arange(N1)
    phases = 2.0 * math.pi / NCH * ((q[:, None] * a[None, :]) % NCH)
    return np.stack([np.cos(phases), sign * np.sin(phases)]).astype(np.float32)


def cosine_table():
    j = np.arange(NB)
    phases = math.pi / (2 * NB) * ((j[:, None] * (2 * j[None, :] + 1)) % (4 * NB))
    weight = np.where(j == 0, (1.0 / NB) ** 0.5, (2.0 / NB) ** 0.5)
    return (np.cos(phases) * weight[:, None]).astype(np.float32)


def band_weights(band_edges, freq):
    bounds = band_edges.astype(jnp.float32)
    freq = freq.astype(jnp.float32)[None, :]
    low, middle, high = bounds[:-2, None], bounds[1:-1, None], bounds[2:, None]
    rising = (freq - low) / (middle - low)
    falling = (high - freq) / (high - middle)
    return jnp.maximum(jnp.minimum(rising, falling), 0.0).astype(jnp.bfloat16)


def interval(band_edges, freq):
    below = jnp.sum((band_edges[None, :] <= freq[:, None]).astype(jnp.int32), axis=1)
    return jnp.minimum(below - 1, NB)


def spectrum_kernel(
    chunks,
    parts,
    table_hbm,
    traces_hbm,
    out_hbm,
    table,
    traces,
    out,
    table_sem,
    traces_sem,
    out_sem,
):
    rows = 2 * BINS
    height = 2 * NF // parts
    across = PLACES["x"] // parts
    lanes = SHARE * N1
    cores = PLACES["core"]
    width = SHARE * FLEN

    def table_copy(j):
        at = pl.ds(j * height, height)
        return pltpu.make_async_copy(table_hbm.at[at], table.at[at], table_sem.at[j])

    def traces_copy(i, core):
        at = pl.ds((i * cores + core) * width, width)
        return pltpu.make_async_copy(
            traces_hbm.at[:, at], traces.at[i, core], traces_sem.at[i, core]
        )

    def out_copy(i, j):
        at = (slice(None), slice(None), slice(None), pl.ds(j * across, across), i)
        return pltpu.make_async_copy(out.at[at], out_hbm.at[at], out_sem.at[i, j])

    traces_copy(0, 0).start()
    table_copy(0).start()
    traces_copy(0, 1).start()
    for j in range(1, parts):
        table_copy(j).start()
    for i in range(1, chunks):
        for core in range(cores):
            traces_copy(i, core).start()
    for i in range(chunks):
        for core in range(cores):
            traces_copy(i, core).wait()
        samples = jnp.concatenate(
            [
                traces[i, core, :, m * FLEN : (m + 1) * FLEN]
                for core in range(cores)
                for m in range(SHARE)
            ],
            axis=0,
        )
        for j in range(parts):
            if i == 0:
                table_copy(j).wait()
            part = lax.dot_general(
                table[j * height : (j + 1) * height, :],
                samples,
                (((1,), (1,)), ((), ())),
                preferred_element_type=jnp.float32,
            ).astype(jnp.bfloat16)
            for k in range(height // rows):
                block = j * (height // rows) + k
                x, zl, y = block // 8, block // 4 % 2, block % 4
                for core in range(cores):
                    out[zl, y, core, x, i] = part[
                        k * rows : (k + 1) * rows, core * lanes : (core + 1) * lanes
                    ]
            out_copy(i, j).start()
    for i in range(chunks):
        for j in range(parts):
            out_copy(i, j).wait()


def sections_kernel(
    cells_ref,
    first_ref,
    second_ref,
    third_ref,
    fourth_ref,
    forward_ref,
    inverse_ref,
    mask_ref,
    bands_ref,
    rounds_ref,
    sums_ref,
    rest_hbm,
    cells,
    turned,
    kept,
    back,
    power_rows,
    sums_f32,
    rest,
    rest_sem,
):
    group = 16
    step = 4
    bf16 = jnp.bfloat16
    dot = functools.partial(jnp.dot, preferred_element_type=jnp.float32)
    fwd_cos, fwd_sin = forward_ref[0], forward_ref[1]
    inv_cos, inv_sin = inverse_ref[0], inverse_ref[1]

    def band_sums(r):
        for m in range(2):
            for g in range(0, N2 // group, 2):
                power = jnp.concatenate(
                    [
                        power_rows[m, :, (g + i) * group : (g + i + 1) * group, :].reshape(
                            BINS * group, N1
                        )
                        for i in range(2)
                    ],
                    axis=1,
                )
                sums = dot(bands_ref[r], power)
                for i in range(2):
                    sums_f32[
                        (g + i) * group : (g + i + 1) * group, m * ROUND : (m + 1) * ROUND, :
                    ] = sums[:, i * N1 : (i + 1) * N1].reshape(group, ROUND, N1)

    for m in range(2):
        for g in range(N2 // group):
            for x in range(2):
                block = cells_ref[
                    g * group : (g + 1) * group,
                    x * BINS : (x + 1) * BINS,
                    m * N1 : (m + 1) * N1,
                ]
                block = jnp.swapaxes(block, 0, 1)
                for f in range(BINS):
                    cells[
                        x * N2 + g * group : x * N2 + (g + 1) * group, f * N1 : (f + 1) * N1
                    ] = block[f]
        for f0 in range(0, BINS, step):
            summed = dot(first_ref[...], cells[:, f0 * N1 : (f0 + step) * N1])
            for i in range(step):
                f = f0 + i
                re = summed[:N2, i * N1 : (i + 1) * N1]
                im = summed[N2:, i * N1 : (i + 1) * N1]
                turned[f * N2 : (f + 1) * N2, :N1] = (re * fwd_cos - im * fwd_sin).astype(bf16)
                turned[f * N2 : (f + 1) * N2, N1:] = (re * fwd_sin + im * fwd_cos).astype(bf16)
        for f0 in range(0, BINS, step):
            section = dot(turned[f0 * N2 : (f0 + step) * N2, :], second_ref[...]).astype(bf16)
            for i in range(step):
                f = f0 + i
                mask = mask_ref[f]
                for x in range(2):
                    kept[f * N2 : (f + 1) * N2, x * N1 : (x + 1) * N1] = (
                        section[i * N2 : (i + 1) * N2, x * N1 : (x + 1) * N1] * mask
                    )
        for f0 in range(0, BINS, step):
            summed = dot(kept[f0 * N2 : (f0 + step) * N2, :], third_ref[...])
            for i in range(step):
                f = f0 + i
                re = summed[i * N2 : (i + 1) * N2, :N1]
                im = summed[i * N2 : (i + 1) * N2, N1:]
                back[:N2, f * N1 : (f + 1) * N1] = (re * inv_cos - im * inv_sin).astype(bf16)
                back[N2:, f * N1 : (f + 1) * N1] = (re * inv_sin + im * inv_cos).astype(bf16)
        for f0 in range(0, BINS, step):
            filtered = dot(fourth_ref[...], back[:, f0 * N1 : (f0 + step) * N1])
            filtered = filtered.astype(bf16).astype(jnp.float32)
            power = filtered[:N2] * filtered[:N2] + filtered[N2:] * filtered[N2:]
            for i in range(step):
                power_rows[m, f0 + i] = power[:, i * N1 : (i + 1) * N1].astype(bf16)
    band_sums(0)
    sums_ref[...] = sums_f32[...].astype(bf16)
    at = pl.ds(pl.multiple_of(pl.program_id(0) * 2 * ROUND, 2 * ROUND), 2 * ROUND)
    for r in range(1, ROUNDS):

        @pl.when(rounds_ref[0] > r)
        def _():
            band_sums(r)
            rest[...] = sums_f32[...].astype(bf16)
            copy = pltpu.make_async_copy(rest, rest_hbm.at[r - 1, :, at, :], rest_sem)
            copy.start()
            copy.wait()


def shares_beside(received):
    sizes = tuple(PLACES[name] for name in ORDER)
    received = received.reshape(*sizes, SHARE * ROUND, N1)
    parts = [
        received[:, :, core, :, zh].reshape(BLOCKS * SHARE * ROUND, N1)
        for zh in range(PLACES["zh"])
        for core in range(PLACES["core"])
    ]
    return jnp.concatenate(parts, axis=1)


def band_places(firsts, r):
    band = firsts[:, None] + r * ROUND + jnp.arange(ROUND, dtype=jnp.int32)
    same = band[None, None, :, None, :] == jnp.arange(NB)[None, :, None, None, None]
    frames = jnp.eye(SHARE, dtype=bool)[:, None, None, :, None]
    return (same & frames).astype(jnp.bfloat16).reshape(SHARE * NB, BLOCKS * SHARE * ROUND)


def cepstra_kernel(sums_ref, places_ref, rest_ref, cosine_ref, out_ref):
    energy = jnp.dot(
        places_ref[...], shares_beside(sums_ref[...]), preferred_element_type=jnp.float32
    )
    logs = jnp.log(jnp.maximum(energy + rest_ref[...], energy_floor))
    width = SHARES * N1
    logs = jnp.concatenate([logs[m * NB : (m + 1) * NB] for m in range(SHARE)], axis=1)
    bf16 = jnp.bfloat16
    dot = functools.partial(jnp.dot, preferred_element_type=jnp.float32)
    high = logs.astype(bf16)
    low = (logs - high.astype(jnp.float32)).astype(bf16)
    cosine = cosine_ref[...]
    cosine_high = cosine.astype(bf16)
    cosine_low = (cosine - cosine_high.astype(jnp.float32)).astype(bf16)
    left = jnp.concatenate([cosine_high, cosine_low, cosine_high], axis=1)
    right = jnp.concatenate([high, high, low], axis=0)
    cepstra = dot(left, right)
    for m in range(SHARE):
        for share in range(SHARES):
            at = m * width + share * N1
            out_ref[share * SHARE + m] = cepstra[:, at : at + N1]


def whole(shape):
    return pl.BlockSpec(shape, lambda i: (0,) * len(shape))


VMEM_LIMIT = 48 * 1024 * 1024
VMEM_WHOLE = 60 * 1024 * 1024


def shards(traces, fan_mask, band_edges):
    devices = math.prod(lax.axis_size(name) for name in PLACES)
    sizes = tuple(PLACES[name] for name in ORDER)
    rows = 2 * BINS
    lanes = SHARE * N1
    order = np.concatenate([listed(), N2 + listed()])
    bf16 = jnp.bfloat16
    params = pltpu.CompilerParams(vmem_limit_bytes=VMEM_LIMIT)

    chunks, parts = PLACES["zh"], 2
    spectrum = pl.pallas_call(
        functools.partial(spectrum_kernel, chunks, parts),
        in_specs=[pl.BlockSpec(memory_space=pltpu.HBM)] * 2,
        out_specs=pl.BlockSpec(memory_space=pltpu.HBM),
        out_shape=jax.ShapeDtypeStruct((*sizes, rows, lanes), bf16),
        scratch_shapes=[
            pltpu.VMEM((2 * NF, FLEN), bf16),
            pltpu.VMEM((chunks, PLACES["core"], N1, SHARE * FLEN), bf16),
            pltpu.VMEM((*sizes, rows, lanes), bf16),
            pltpu.SemaphoreType.DMA((parts,)),
            pltpu.SemaphoreType.DMA((chunks, PLACES["core"])),
            pltpu.SemaphoreType.DMA((chunks, parts)),
        ],
        compiler_params=pltpu.CompilerParams(vmem_limit_bytes=VMEM_WHOLE),
        name="spectrum",
    )(jnp.asarray(time_table()), traces)
    spectrum = spectrum.reshape(devices, rows, lanes)

    cells = lax.all_to_all(spectrum, ORDER, split_axis=0, concat_axis=0, tiled=True)

    mask = jnp.transpose(fan_mask.reshape(BINS, N1, N2), (0, 2, 1))
    mask = (mask > 0).astype(bf16)

    blocks = np.arange(BLOCKS, dtype=np.int32).reshape(
        PLACES["x"], PLACES["zl"], PLACES["y"]
    )
    starts = jnp.asarray(blocks.transpose(1, 2, 0).reshape(-1) * BINS)
    firsts = interval(band_edges, starts) - 1
    touched = interval(band_edges, starts + BINS - 1) + 1 - firsts
    rounds = (jnp.max(touched) + ROUND - 1) // ROUND
    own = lax.axis_index(("x", "zl", "y"))
    weights = band_weights(band_edges, own * BINS + jnp.arange(BINS, dtype=jnp.int32))
    own_first = interval(band_edges, jnp.reshape(own * BINS, (1,))) - 1
    sent = own_first + jnp.arange(ROUNDS * ROUND, dtype=jnp.int32)
    chosen = sent[:, None] == jnp.arange(NB, dtype=jnp.int32)[None, :]
    weights = jnp.max(
        jnp.where(chosen[:, :, None], weights[None], jnp.zeros((), bf16)), axis=1
    )
    weights = weights.reshape(ROUNDS, 1, ROUND, BINS, 1)
    same = jnp.eye(16, dtype=bool)[None, :, None, None, :]
    bands = jnp.where(same, weights, jnp.zeros((), bf16)).reshape(
        ROUNDS, 16 * ROUND, BINS * 16
    )

    sums, rest = pl.pallas_call(
        sections_kernel,
        grid=(SHARE // 2,),
        in_specs=[
            pl.BlockSpec((N2, rows, 2 * N1), lambda i: (0, 0, i)),
            whole((2 * N2, 2 * N2)),
            whole((2 * N1, 2 * N1)),
            whole((2 * N1, 2 * N1)),
            whole((2 * N2, 2 * N2)),
            whole((2, N2, N1)),
            whole((2, N2, N1)),
            whole((BINS, N2, N1)),
            whole((ROUNDS, 16 * ROUND, BINS * 16)),
            pl.BlockSpec(memory_space=pltpu.SMEM),
        ],
        out_specs=[
            pl.BlockSpec((N2, 2 * ROUND, N1), lambda i: (0, i, 0)),
            pl.BlockSpec(memory_space=pltpu.HBM),
        ],
        out_shape=[
            jax.ShapeDtypeStruct((N2, SHARE * ROUND, N1), bf16),
            jax.ShapeDtypeStruct((ROUNDS - 1, N2, SHARE * ROUND, N1), bf16),
        ],
        scratch_shapes=[
            pltpu.VMEM((2 * N2, BINS * N1), bf16),
            pltpu.VMEM((BINS * N2, 2 * N1), bf16),
            pltpu.VMEM((BINS * N2, 2 * N1), bf16),
            pltpu.VMEM((2 * N2, BINS * N1), bf16),
            pltpu.VMEM((2, BINS, N2, N1), bf16),
            pltpu.VMEM((N2, 2 * ROUND, N1), jnp.float32),
            pltpu.VMEM((N2, 2 * ROUND, N1), bf16),
            pltpu.SemaphoreType.DMA,
        ],
        compiler_params=params,
        name="sections",
    )(
        cells,
        jnp.asarray(left_table(N2, -1.0)[:, order]),
        jnp.asarray(right_table(N1, -1.0)),
        jnp.asarray(right_table(N1, 1.0)),
        jnp.asarray(left_table(N2, 1.0)[order]),
        jnp.asarray(twiddle(-1.0)),
        jnp.asarray(twiddle(1.0)),
        mask,
        bands,
        jnp.reshape(rounds, (1,)),
    )

    def send(sums):
        return lax.all_to_all(sums, ORDER, split_axis=0, concat_axis=0, tiled=True)

    def further_round(r, energy):
        received = send(lax.dynamic_index_in_dim(rest, r - 1, 0, keepdims=False))
        return energy + jnp.dot(
            band_places(firsts, r), shares_beside(received), preferred_element_type=jnp.float32
        )

    further = lax.fori_loop(
        1, rounds, further_round, jnp.zeros((SHARE * NB, SHARES * N1), jnp.float32)
    )
    return pl.pallas_call(
        cepstra_kernel,
        in_specs=[pl.BlockSpec(memory_space=pltpu.VMEM)] * 4,
        out_specs=pl.BlockSpec(memory_space=pltpu.VMEM),
        out_shape=jax.ShapeDtypeStruct((FRAMES, NB, N1), jnp.float32),
        compiler_params=params,
        name="cepstra",
    )(send(sums), band_places(firsts, 0), further, jnp.asarray(cosine_table()))


def solution(mesh):
    places = Mesh(mesh.devices.reshape(tuple(PLACES.values())), tuple(PLACES))
    whole_axes = tuple(PLACES)
    in_specs = (P(whole_axes, None), P(("x", "zl", "y"), None), P())
    out_specs = P(None, None, whole_axes)
    return jax.shard_map(
        shards, mesh=places, in_specs=in_specs, out_specs=out_specs, check_vma=False
    )
```
